256 devices in a mesh: dp: 128 (over z, x, y), sub: 2 (over core).
Axes of the slice: x: 4, y: 4, z: 8, core: 2. Of those that a mesh axis runs over, the one named last changes fastest.
Arguments:
- queries: bfloat16 [49152, 4096], P('dp', 'sub'), may hold values from -32 to 32
- passages: bfloat16 [49152, 4096], P('dp', 'sub'), may hold values from -8 to 8
- positive: int32 [128, 384], P('dp'), may hold values from 0 to 383, each once within a row
- pair_on: int32 [128, 3], replicated, may hold values from 0 to 1, as said below
Outputs:
- loss: float32 [1], replicated
- query_grad: float32 [49152, 4096], P('dp', 'sub')
- passage_grad: float32 [49152, 4096], P('dp', 'sub')
The draws below stay inside these ranges and needn't reach their ends.
Inputs may be any that keep to these rules, and one draw needn't show every extreme that they name: pair_on[s, k] equals pair_on[s xor 2 ** (log2(128) - 3 + k), k]; shards 0 and 2 ** (log2(128) - 3) - 1 pair at every level.
All inputs are finite; a program needn't handle non-finite values.
Results may differ from the reference program's by a relative error of at most 0.0016.
Values may be sent and summed in bfloat16 or wider, within the bound.
A program may use at most 128 MiB of HBM per device.

```python
import math
import jax
import jax.numpy as jnp
from jax import lax

D = 4096
R = 384
PB = 3
TOTAL = 49152
N_DP = 128


def draw_queries(key, part):
    key = jax.random.fold_in(key, 1)
    values = jnp.clip(jax.random.normal(key, (TOTAL, D), jnp.float32), -6.0, 6.0)
    return values.astype(jnp.bfloat16)


def draw_passages(key, part):
    key = jax.random.fold_in(key, 2)
    values = jnp.clip(jax.random.normal(key, (TOTAL, D), jnp.float32), -6.0, 6.0)
    return values.astype(jnp.bfloat16)


def draw_pair_on(key, part):
    key = jax.random.fold_in(key, 3)
    depth = N_DP.bit_length() - 1
    coins = jax.random.randint(key, (N_DP, PB), 0, 2)
    coins = coins.at[0].set(1)
    coins = coins.at[(1 << depth - PB) - 1].set(1)
    shards = jnp.arange(N_DP, dtype=jnp.int32)[:, None]
    masks = jnp.array([1 << depth - PB + k for k in range(PB)], jnp.int32)[None, :]
    base_rows = jnp.bitwise_and(shards, jnp.bitwise_not(masks))
    levels = jnp.arange(PB, dtype=jnp.int32)[None, :]
    return coins[base_rows, levels].astype(jnp.int32)


def setup_inputs(seed: int = 0) -> dict:
    key_list = jax.random.split(jax.random.key(seed), 5)
    queries = draw_queries(jax.random.fold_in(key_list[4], 71), 0)
    passages = draw_passages(jax.random.fold_in(key_list[4], 71), 0)
    positive = jax.vmap(lambda own: jax.random.permutation(own, R))(jax.random.split(key_list[2], N_DP)).reshape((N_DP, R)).astype(jnp.int32)
    pair_on = draw_pair_on(jax.random.fold_in(key_list[4], 71), 0)
    return dict(queries=queries, passages=passages, positive=positive, pair_on=pair_on)


def tile_logits(left, right):
    return lax.dot_general(left, right, (((1,), (1,)), ((), ())), preferred_element_type=jnp.float32) / math.sqrt(D)

def lse_axis(values, axis):
    return jax.scipy.special.logsumexp(values, axis=axis)

def reference(queries, passages, positive, pair_on):
    depth = N_DP.bit_length() - 1
    query_blocks = queries.reshape(N_DP, R, D)
    passage_blocks = passages.reshape(N_DP, R, D)
    level_bits = jnp.array([1 << depth - PB + k for k in range(PB)], jnp.int32)
    columns = jnp.arange(R, dtype=jnp.int32)

    def first_pass(shard):
        mine_q = query_blocks[shard]
        mine_p = passage_blocks[shard]
        own = tile_logits(mine_q, mine_p)
        row = lse_axis(own, 1)
        col = lse_axis(own, 0)
        for k in range(PB):
            other = jnp.bitwise_xor(shard, level_bits[k])
            active = pair_on[shard, k] > 0
            upper = tile_logits(mine_q, passage_blocks[other])
            lower = tile_logits(query_blocks[other], mine_p)
            row = jnp.where(active, jnp.logaddexp(row, lse_axis(upper, 1)), row)
            col = jnp.where(active, jnp.logaddexp(col, lse_axis(lower, 0)), col)
        onehot = (positive[shard][:, None] == columns[None, :]).astype(jnp.float32)
        return (row, col, jnp.sum(own * onehot))
    rows_lse, cols_lse, pos_sums = lax.map(first_pass, jnp.arange(N_DP, dtype=jnp.int32))

    def second_pass(shard):
        mine_q = query_blocks[shard]
        mine_p = passage_blocks[shard]
        own = tile_logits(mine_q, mine_p)
        onehot = (positive[shard][:, None] == columns[None, :]).astype(jnp.float32)
        grad = (jnp.exp(own - rows_lse[shard][:, None]) + jnp.exp(own - cols_lse[shard][None, :]) - 2.0 * onehot).astype(jnp.bfloat16)
        dq = jnp.dot(grad, mine_p, preferred_element_type=jnp.float32)
        dp = lax.dot_general(grad, mine_q, (((0,), (0,)), ((), ())), preferred_element_type=jnp.float32)
        for k in range(PB):
            other = jnp.bitwise_xor(shard, level_bits[k])
            active = pair_on[shard, k] > 0
            far_q = query_blocks[other]
            far_p = passage_blocks[other]
            upper = tile_logits(mine_q, far_p)
            lower = tile_logits(far_q, mine_p)
            g_up = jnp.exp(upper - rows_lse[shard][:, None]) + jnp.exp(upper - cols_lse[other][None, :])
            g_low = jnp.exp(lower - rows_lse[other][:, None]) + jnp.exp(lower - cols_lse[shard][None, :])
            g_up = jnp.where(active, g_up, 0.0).astype(jnp.bfloat16)
            g_low = jnp.where(active, g_low, 0.0).astype(jnp.bfloat16)
            dq = dq + jnp.dot(g_up, far_p, preferred_element_type=jnp.float32)
            dp = dp + lax.dot_general(g_low, far_q, (((0,), (0,)), ((), ())), preferred_element_type=jnp.float32)
        return (dq, dp)
    dq_all, dp_all = lax.map(second_pass, jnp.arange(N_DP, dtype=jnp.int32))
    total = jnp.sum(rows_lse) + jnp.sum(cols_lse) - 2.0 * jnp.sum(pos_sums)
    loss = jnp.reshape(total / (2.0 * TOTAL), (1,))
    return (loss, dq_all.reshape(TOTAL, D), dp_all.reshape(TOTAL, D))
```

```python
import functools
import math

import jax
import jax.numpy as jnp
from jax import lax
from jax.experimental import pallas as pl
from jax.experimental.pallas import tpu as pltpu
from jax.sharding import PartitionSpec as P

MESH = pl.DeviceIdType.MESH
NZ = 8
LEVELS = 3
CHUNKS = 8
F32 = jnp.float32
BF16 = jnp.bfloat16

P_UP0, P_UP1, P_UP2, P_DN0, P_DN1, P_OWN = range(6)
Q_UP0, Q_UP1, Q_DN0, Q_DN1, Q_DN2, Q_OWN = range(6)
T_OWN, T_U0, T_L0, T_X = 0, 1, 4, 7


def dot_nt(a, b):
    return lax.dot_general(a, b, (((1,), (1,)), ((), ())), preferred_element_type=F32)


def dot_nn(a, b):
    return jnp.dot(a, b, preferred_element_type=F32)


def to_lanes(column):
    rows = column.shape[0]
    return jnp.transpose(jnp.broadcast_to(column, (rows, 128)))[0:1, :]


def to_column(lanes):
    rows = lanes.shape[1]
    return jnp.transpose(jnp.broadcast_to(lanes, (128, rows)))[:, 0:1]


def lse_rows(tile):
    top = jnp.max(tile, axis=1, keepdims=True)
    return top + jnp.log(jnp.sum(jnp.exp(tile - top), axis=1, keepdims=True))


def lse_cols(tile):
    top = jnp.max(tile, axis=0, keepdims=True)
    return top + jnp.log(jnp.sum(jnp.exp(tile - top), axis=0, keepdims=True))


def kernel(
    nx, ny, scale, count,
    q_hbm, p_hbm, pos_ref, pair_ref,
    loss_ref, dq_hbm, dp_hbm,
    pb, qb, cin, cs, cm, part, got, dqv, dpv,
    g_own, g_own_t, g_up, g_up0_t, g_low, g_x,
    ms1, mr1, ms2, mr2, lz, lx, ly,
    own_sem, out_sem,
    p_send_up, p_send_dn, p_recv,
    q_send_up, q_send_dn, q_recv,
    c_send, c_recv,
    t_send, t_recv,
    m1_send, m1_recv, m2_send, m2_recv,
    z_send, z_recv, x_send, x_recv, y_send, y_recv,
):
    rows = pb.shape[2]
    width = pb.shape[3]
    per_z = nx * ny
    dp = lax.axis_index("dp")
    sub = lax.axis_index("sub")
    z = dp // per_z
    xy = dp % per_z
    x = xy // ny
    y = xy % ny
    role = z % 4
    second = role // 2
    sign = 1 - 2 * second
    outer = (role % 3) == 0
    inner = jnp.logical_not(outer)

    def at_z(other):
        return (((other + 2 * NZ) % NZ) * per_z + xy, sub)

    up = at_z(z + sign)
    down = at_z(z - sign)
    twin = (dp, 1 - sub)

    def partner_z(level):
        step = 1 << level
        return z + step - 2 * step * ((z // step) % 2)

    partners = [at_z(partner_z(level)) for level in range(LEVELS)]
    far2 = at_z(z - 2 * sign)

    def remote(src, dst, send, recv, device):
        return pltpu.make_async_remote_copy(
            src_ref=src, dst_ref=dst, send_sem=send, recv_sem=recv,
            device_id=device, device_id_type=MESH,
        )

    def p_up(i, src, dst, k):
        return remote(pb.at[src, k], pb.at[dst, k], p_send_up.at[i, k], p_recv.at[dst, k], up)

    def p_dn(i, src, dst, k):
        return remote(pb.at[src, k], pb.at[dst, k], p_send_dn.at[i, k], p_recv.at[dst, k], down)

    def q_up(i, src, dst, k):
        return remote(qb.at[src, k], qb.at[dst, k], q_send_up.at[i, k], q_recv.at[dst, k], up)

    def q_dn(i, src, dst, k):
        return remote(qb.at[src, k], qb.at[dst, k], q_send_dn.at[i, k], q_recv.at[dst, k], down)

    def c_up(k):
        return remote(cs.at[k], cin.at[k], c_send.at[0, k], c_recv.at[k], up)

    def c_dn(k):
        return remote(cm.at[k], cin.at[k], c_send.at[1, k], c_recv.at[k], down)

    def p_wait(slot, k):
        remote(pb.at[slot, k], pb.at[slot, k], p_send_up.at[0, k], p_recv.at[slot, k], up).wait_recv()

    def q_wait(slot, k):
        remote(qb.at[slot, k], qb.at[slot, k], q_send_up.at[0, k], q_recv.at[slot, k], up).wait_recv()

    def tile_copy(i):
        return remote(part.at[i], got.at[i], t_send.at[i], t_recv.at[i], twin)

    def finish_tile(i):
        tile_copy(i).wait_recv()
        got[i] = (got[i] + part[i]) * scale

    def m1_copy(level):
        return remote(ms1.at[level], mr1.at[level], m1_send.at[level], m1_recv.at[level], partners[level])

    def m2_copy(i):
        device = partners[i] if i < LEVELS else far2
        return remote(ms2, mr2.at[i], m2_send.at[i], m2_recv.at[i], device)

    def z_copy(d):
        return remote(lz.at[z], lz.at[z], z_send.at[d], z_recv.at[z], at_z(z + d))

    def z_wait(d):
        other = (z + d) % NZ
        remote(lz.at[other], lz.at[other], z_send.at[d], z_recv.at[other], at_z(z + d)).wait_recv()

    def x_device(d):
        return (z * per_z + ((x + d) % nx) * ny + y, sub)

    def x_copy(d):
        return remote(lx.at[x], lx.at[x], x_send.at[d], x_recv.at[x], x_device(d))

    def x_wait(d):
        other = (x + d) % nx
        remote(lx.at[other], lx.at[other], x_send.at[d], x_recv.at[other], x_device(d)).wait_recv()

    def y_device(d):
        return (z * per_z + x * ny + (y + d) % ny, sub)

    def y_copy(d):
        return remote(ly.at[y], ly.at[y], y_send.at[d], y_recv.at[y], y_device(d))

    def y_wait(d):
        other = (y + d) % ny
        remote(ly.at[other], ly.at[other], y_send.at[d], y_recv.at[other], y_device(d)).wait_recv()

    def load_p(k):
        return pltpu.make_async_copy(
            p_hbm.at[:, pl.ds(pl.multiple_of(k * width, width), width)], pb.at[P_OWN, k], own_sem.at[0, k]
        )

    def load_q(k):
        return pltpu.make_async_copy(
            q_hbm.at[:, pl.ds(pl.multiple_of(k * width, width), width)], qb.at[Q_OWN, k], own_sem.at[1, k]
        )

    def store_dq(k):
        return pltpu.make_async_copy(
            dqv.at[k], dq_hbm.at[:, pl.ds(pl.multiple_of(k * width, width), width)], out_sem.at[0, k]
        )

    def store_dp(k):
        return pltpu.make_async_copy(
            dpv.at[k], dp_hbm.at[:, pl.ds(pl.multiple_of(k * width, width), width)], out_sem.at[1, k]
        )

    def each_chunk(body):
        def step(k, carry):
            body(k)
            return carry

        lax.fori_loop(0, CHUNKS, step, 0)

    def add_tile(i, k, left, right):
        @pl.when(k == 0)
        def _():
            part[i] = dot_nt(left, right)

        @pl.when(k > 0)
        def _():
            part[i] = part[i] + dot_nt(left, right)

    @each_chunk
    def _(k):
        load_p(k).start()

    @each_chunk
    def _(k):
        load_q(k).start()

    barrier = pltpu.get_barrier_semaphore()
    greeted = [twin]
    greeted += [at_z(z + d) for d in range(1, NZ)]
    greeted += [x_device(d) for d in range(1, nx)]
    greeted += [y_device(d) for d in range(1, ny)]
    for device in greeted:
        pl.semaphore_signal(barrier, inc=1, device_id=device, device_id_type=MESH)
    pl.semaphore_wait(barrier, len(greeted))

    @each_chunk
    def _(k):
        load_p(k).wait()

        @pl.when(outer)
        def _():
            p_up(0, P_OWN, P_DN0, k).start()

        @pl.when(inner)
        def _():
            p_up(0, P_OWN, P_UP0, k).start()
            p_dn(0, P_OWN, P_UP0, k).start()

    @each_chunk
    def _(k):
        load_q(k).wait()

        @pl.when(outer)
        def _():
            q_dn(0, Q_OWN, Q_DN2, k).start()

    @each_chunk
    def _(k):
        add_tile(T_OWN, k, pb[P_OWN, k], qb[Q_OWN, k])

    tile_copy(T_OWN).start()

    near = jnp.where(outer, P_UP0, P_DN0)

    @each_chunk
    def _(k):
        @pl.when(inner)
        def _():
            p_wait(P_UP0, k)
            p_dn(1, P_UP0, P_UP1, k).start()

        p_wait(near, k)

        @pl.when(inner)
        def _():
            p_up(1, P_DN0, P_UP1, k).start()

        add_tile(T_U0, k, qb[Q_OWN, k], pb[near, k])

    tile_copy(T_U0).start()

    @each_chunk
    def _(k):
        p_wait(P_UP1, k)

        @pl.when(outer)
        def _():
            p_dn(0, P_UP1, P_DN0, k).start()

        @pl.when(inner)
        def _():
            p_dn(2, P_UP1, P_UP2, k).start()

        add_tile(T_U0 + 1, k, qb[Q_OWN, k], pb[P_UP1, k])

        @pl.when(outer)
        def _():
            p_wait(P_DN0, k)
            p_up(1, P_DN0, P_DN1, k).start()

    tile_copy(T_U0 + 1).start()

    @each_chunk
    def _(k):
        @pl.when(outer)
        def _():
            q_wait(Q_DN2, k)
            q_up(0, Q_DN2, Q_DN2, k).start()

        @pl.when(inner)
        def _():
            q_up(0, Q_OWN, Q_UP0, k).start()

    @each_chunk
    def _(k):
        @pl.when(outer)
        def _():
            p_wait(P_UP2, k)
            p_dn(1, P_UP2, P_DN1, k).start()

        p_wait(P_DN1, k)
        add_tile(T_U0 + 2, k, qb[Q_OWN, k], pb[P_DN1, k])

        @pl.when(inner)
        def _():
            q_wait(Q_DN2, k)
            add_tile(T_X, k, pb[P_UP1, k], qb[Q_DN2, k])

    tile_copy(T_U0 + 2).start()

    @pl.when(inner)
    def _():
        tile_copy(T_X).start()

    def q_first(k):
        @pl.when(outer)
        def _():
            q_up(1, Q_OWN, Q_DN0, k).start()

        @pl.when(inner)
        def _():
            q_wait(Q_UP0, k)
            q_dn(0, Q_UP0, Q_UP1, k).start()

    low = jnp.where(outer, T_L0 + 1, T_L0)
    q_near = jnp.where(outer, Q_UP1, Q_DN0)

    def q_relay(k):
        q_wait(q_near, k)

        @pl.when(outer)
        def _():
            q_dn(1, Q_UP1, Q_DN0, k).start()

        @pl.when(inner)
        def _():
            q_up(1, Q_DN0, Q_UP1, k).start()

        if k + 2 < CHUNKS:
            q_first(k + 2)
        tile = dot_nt(pb[P_OWN, k], qb[q_near, k])
        part[low] = tile if k == 0 else part[low] + tile

    active = [pair_ref[dp, level] > 0 for level in range(LEVELS)]
    x_active = pair_ref[partner_z(1) * per_z + xy, 2] > 0
    hit = (pos_ref[...] == lax.broadcasted_iota(jnp.int32, (rows, rows), 0)).astype(F32)

    def up_stats(level):
        finish_tile(T_U0 + level)
        tile = got[T_U0 + level]
        ms1[level] = jnp.broadcast_to(lse_cols(tile), (8, rows))
        m1_copy(level).start()
        return to_lanes(lse_rows(tile))

    def gather(parts):
        parts = [parts[0]] + [jnp.where(a, v, -jnp.inf) for a, v in zip(active, parts[1:])]
        top = functools.reduce(jnp.maximum, parts)
        return top + jnp.log(functools.reduce(jnp.add, [jnp.exp(v - top) for v in parts]))

    q_first(0)
    q_first(1)
    finish_tile(T_OWN)
    own_rows = lse_cols(got[T_OWN])
    own_cols = to_lanes(lse_rows(got[T_OWN]))
    row_parts = [own_rows, up_stats(0), up_stats(1)]
    q_relay(0)
    row_parts.append(up_stats(2))
    q_relay(1)
    q_relay(2)
    for level in range(LEVELS):
        m1_copy(level).wait_recv()
    row_lse = gather(row_parts)
    col_lse = gather([own_cols] + [mr1[level][0:1, :] for level in range(LEVELS)])
    ms2[0:4, :] = jnp.broadcast_to(row_lse, (4, rows))
    ms2[4:8, :] = jnp.broadcast_to(col_lse, (4, rows))
    for level in range(LEVELS):
        m2_copy(level).start()

    @pl.when(outer)
    def _():
        m2_copy(LEVELS).start()

    share = jnp.sum(row_lse) + jnp.sum(col_lse) - 2.0 * jnp.sum(got[T_OWN] * hit)
    lz[z] = jnp.full((8, 128), share, F32)
    for d in range(1, NZ):
        z_copy(d).start()
    q_relay(3)
    row_column = to_column(row_lse)
    col_column = to_column(col_lse)
    grad_t = jnp.exp(got[T_OWN] - row_lse) + jnp.exp(got[T_OWN] - col_column) - 2.0 * hit
    g_own_t[...] = grad_t.astype(BF16)
    g_own[...] = jnp.transpose(grad_t).astype(BF16)
    q_relay(4)
    q_relay(5)

    for level in range(LEVELS):
        m2_copy(level).wait_recv()

    def up_grad(level):
        tile = got[T_U0 + level]
        grad = jnp.exp(tile - row_column) + jnp.exp(tile - mr2[level][4:5, :])
        return jnp.where(active[level], grad, 0.0)

    @pl.when(inner)
    def _():
        m2_copy(LEVELS).wait_recv()
        finish_tile(T_X)
        tile = got[T_X]
        grad = jnp.exp(tile - mr2[LEVELS][0:1, :]) + jnp.exp(tile - to_column(mr2[1][4:5, :]))
        g_x[...] = jnp.where(x_active, grad, 0.0).astype(BF16)

    grad0 = up_grad(0)
    g_up[0] = grad0.astype(BF16)
    g_up0_t[...] = jnp.transpose(grad0).astype(BF16)
    q_relay(6)
    g_up[1] = up_grad(1).astype(BF16)
    q_relay(7)
    tile_copy(low).start()
    g_up[2] = up_grad(2).astype(BF16)

    @each_chunk
    def _(k):
        @pl.when(inner)
        def _():
            cs[k] = dot_nn(g_x[...], qb[Q_DN2, k]).astype(BF16)
            c_up(k).start()

        @pl.when(outer)
        def _():
            q_wait(Q_DN0, k)
            q_up(2, Q_DN0, Q_DN1, k).start()

    def low_grad(level):
        finish_tile(T_L0 + level)
        tile = got[T_L0 + level]
        grad = jnp.exp(tile - mr2[level][0:1, :]) + jnp.exp(tile - col_column)
        g_low[level] = jnp.where(active[level], grad, 0.0).astype(BF16)

    for d in range(1, NZ):
        z_wait(d)
    lx[x] = functools.reduce(jnp.add, [lz[i] for i in range(NZ)])
    for d in range(1, nx):
        x_copy(d).start()

    @each_chunk
    def _(k):
        @pl.when(inner)
        def _():
            remote(cs.at[k], cin.at[k], c_send.at[0, k], c_recv.at[k], up).wait_recv()
            cm[k] = (cin[k].astype(F32) + dot_nn(g_up0_t[...], qb[Q_OWN, k])).astype(BF16)
            c_dn(k).start()

        total = dot_nn(g_own[...], pb[P_OWN, k])
        total = total + dot_nn(g_up[0], pb[near, k])
        total = total + dot_nn(g_up[1], pb[P_UP1, k])
        total = total + dot_nn(g_up[2], pb[P_DN1, k])
        dqv[k] = total
        store_dq(k).start()

        @pl.when(inner)
        def _():
            q_wait(Q_UP1, k)
            add_tile(T_L0 + 1, k, pb[P_OWN, k], qb[Q_UP1, k])

    for d in range(1, nx):
        x_wait(d)
    ly[y] = functools.reduce(jnp.add, [lx[i] for i in range(nx)])
    for d in range(1, ny):
        y_copy(d).start()

    @pl.when(outer)
    def _():
        low_grad(1)

        @each_chunk
        def _(k):
            dpv[k] = dot_nn(g_own_t[...], qb[Q_OWN, k]) + dot_nn(g_low[1], qb[Q_UP1, k])

        @each_chunk
        def _(k):
            remote(cs.at[k], cin.at[k], c_send.at[0, k], c_recv.at[k], up).wait_recv()
            dpv[k] = dpv[k] + cin[k].astype(F32)
            store_dp(k).start()

    @pl.when(inner)
    def _():
        tile_copy(T_L0 + 1).start()
        low_grad(0)

        @each_chunk
        def _(k):
            q_wait(Q_DN1, k)
            add_tile(T_L0 + 2, k, pb[P_OWN, k], qb[Q_DN1, k])

        tile_copy(T_L0 + 2).start()
        low_grad(1)

        @each_chunk
        def _(k):
            total = dot_nn(g_own_t[...], qb[Q_OWN, k])
            total = total + dot_nn(g_low[0], qb[Q_DN0, k])
            dpv[k] = total + dot_nn(g_low[1], qb[Q_UP1, k])

        low_grad(2)

        @each_chunk
        def _(k):
            dpv[k] = dpv[k] + dot_nn(g_low[2], qb[Q_DN1, k])
            store_dp(k).start()

    for d in range(1, ny):
        y_wait(d)
    total_loss = functools.reduce(jnp.add, [ly[i] for i in range(ny)])
    loss_ref[0] = jnp.max(total_loss) / count

    @each_chunk
    def _(k):
        store_dq(k).wait()
        store_dp(k).wait()
        p_up(0, P_OWN, P_DN0, k).wait_send()
        p_up(1, P_DN0, P_DN1, k).wait_send()
        p_dn(0, P_UP1, P_DN0, k).wait_send()
        p_dn(1, P_UP2, P_DN1, k).wait_send()
        q_up(0, Q_DN2, Q_DN2, k).wait_send()
        q_up(1, Q_OWN, Q_DN0, k).wait_send()
        q_dn(0, Q_OWN, Q_DN2, k).wait_send()

        @pl.when(outer)
        def _():
            q_up(2, Q_DN0, Q_DN1, k).wait_send()
            q_dn(1, Q_UP1, Q_DN0, k).wait_send()

        @pl.when(inner)
        def _():
            p_dn(2, P_UP1, P_UP2, k).wait_send()
            c_up(k).wait_send()
            c_dn(k).wait_send()

    tile_copy(T_OWN).wait_send()
    for level in range(LEVELS):
        tile_copy(T_U0 + level).wait_send()
        m1_copy(level).wait_send()
        m2_copy(level).wait_send()
    tile_copy(T_L0 + 1).wait_send()

    @pl.when(outer)
    def _():
        m2_copy(LEVELS).wait_send()

    @pl.when(inner)
    def _():
        tile_copy(T_X).wait_send()
        tile_copy(T_L0).wait_send()
        tile_copy(T_L0 + 2).wait_send()

    for d in range(1, NZ):
        z_copy(d).wait_send()
    for d in range(1, nx):
        x_copy(d).wait_send()
    for d in range(1, ny):
        y_copy(d).wait_send()


def local(nx, ny, queries, passages, positive, pair_on):
    rows, depth = queries.shape
    width = depth // CHUNKS
    full = depth * lax.axis_size("sub")
    count = 2.0 * rows * lax.axis_size("dp")
    dma = pltpu.SemaphoreType.DMA
    block = (CHUNKS, rows, width)
    tile = (rows, rows)
    anywhere = pl.BlockSpec(memory_space=pl.ANY)
    return pl.pallas_call(
        functools.partial(kernel, nx, ny, 1.0 / math.sqrt(full), count),
        out_shape=(
            jax.ShapeDtypeStruct((1,), F32),
            jax.ShapeDtypeStruct((rows, depth), F32),
            jax.ShapeDtypeStruct((rows, depth), F32),
        ),
        in_specs=[
            anywhere,
            anywhere,
            pl.BlockSpec(memory_space=pltpu.VMEM),
            pl.BlockSpec(memory_space=pltpu.SMEM),
        ],
        out_specs=(pl.BlockSpec(memory_space=pltpu.SMEM), anywhere, anywhere),
        scratch_shapes=[
            pltpu.VMEM((6,) + block, BF16),
            pltpu.VMEM((6,) + block, BF16),
            pltpu.VMEM(block, BF16),
            pltpu.VMEM(block, BF16),
            pltpu.VMEM(block, BF16),
            pltpu.VMEM((8,) + tile, F32),
            pltpu.VMEM((8,) + tile, F32),
            pltpu.VMEM(block, F32),
            pltpu.VMEM(block, F32),
            pltpu.VMEM(tile, BF16),
            pltpu.VMEM(tile, BF16),
            pltpu.VMEM((LEVELS,) + tile, BF16),
            pltpu.VMEM(tile, BF16),
            pltpu.VMEM((LEVELS,) + tile, BF16),
            pltpu.VMEM(tile, BF16),
            pltpu.VMEM((LEVELS, 8, rows), F32),
            pltpu.VMEM((LEVELS, 8, rows), F32),
            pltpu.VMEM((8, rows), F32),
            pltpu.VMEM((LEVELS + 1, 8, rows), F32),
            pltpu.VMEM((NZ, 8, 128), F32),
            pltpu.VMEM((nx, 8, 128), F32),
            pltpu.VMEM((ny, 8, 128), F32),
            dma((2, CHUNKS)),
            dma((2, CHUNKS)),
            dma((2, CHUNKS)),
            dma((3, CHUNKS)),
            dma((5, CHUNKS)),
            dma((3, CHUNKS)),
            dma((2, CHUNKS)),
            dma((5, CHUNKS)),
            dma((2, CHUNKS)),
            dma((CHUNKS,)),
            dma((8,)),
            dma((8,)),
            dma((LEVELS,)),
            dma((LEVELS,)),
            dma((LEVELS + 1,)),
            dma((LEVELS + 1,)),
            dma((NZ,)),
            dma((NZ,)),
            dma((nx,)),
            dma((nx,)),
            dma((ny,)),
            dma((ny,)),
        ],
        compiler_params=pltpu.CompilerParams(
            collective_id=1, has_side_effects=True, vmem_limit_bytes=58 << 20
        ),
        name="infonce",
    )(queries, passages, positive, pair_on)


def solution(mesh):
    per_z = mesh.shape["dp"] // NZ
    nx = math.isqrt(per_z)
    ny = per_z // nx
    return jax.shard_map(
        functools.partial(local, nx, ny),
        mesh=mesh,
        in_specs=(P("dp", "sub"), P("dp", "sub"), P("dp", None), P()),
        out_specs=(P(), P("dp", "sub"), P("dp", "sub")),
        check_vma=False,
    )
```

```python
import functools
import math

import jax
import jax.numpy as jnp
from jax import lax
from jax.experimental import pallas as pl
from jax.experimental.pallas import tpu as pltpu
from jax.sharding import PartitionSpec as P

MESH = pl.DeviceIdType.MESH
NZ = 8
LEVELS = 3
CHUNKS = 8
LAG = 2
EARLY = 2
NEAR = 4
F32 = jnp.float32
BF16 = jnp.bfloat16

P_UP0, P_UP1, P_UP2, P_DN0, P_DN1, P_OWN = range(6)
Q_UP0, Q_UP1, Q_DN0, Q_DN1, Q_DN2, Q_OWN = range(6)
T_OWN, T_U0, T_L0, T_X = 0, 1, 4, 7


def dot_nt(a, b):
    return lax.dot_general(a, b, (((1,), (1,)), ((), ())), preferred_element_type=F32)


def dot_nn(a, b):
    return jnp.dot(a, b, preferred_element_type=F32)


def to_lanes(column):
    rows = column.shape[0]
    return jnp.transpose(jnp.broadcast_to(column, (rows, 128)))[0:1, :]


def to_column(lanes):
    rows = lanes.shape[1]
    return jnp.transpose(jnp.broadcast_to(lanes, (128, rows)))[:, 0:1]


def lse_rows(tile):
    top = jnp.max(tile, axis=1, keepdims=True)
    return top + jnp.log(jnp.sum(jnp.exp(tile - top), axis=1, keepdims=True))


def lse_cols(tile):
    top = jnp.max(tile, axis=0, keepdims=True)
    return top + jnp.log(jnp.sum(jnp.exp(tile - top), axis=0, keepdims=True))


def kernel(
    nx, ny, scale, count,
    q_hbm, p_hbm, pos_ref, pair_ref,
    loss_ref, dq_hbm, dp_hbm,
    pb, qb, cin, cs, cm, part, got, dqv, dpv,
    g_own, g_own_t, g_up, g_up0_t, g_low, g_x, lse,
    ms1, mr1, ms2, mr2, lz, lx, ly,
    own_sem, out_sem,
    p_send_up, p_send_dn, p_recv,
    q_send_up, q_send_dn, q_recv,
    c_send, c_recv,
    t_send, t_recv,
    m1_send, m1_recv, m2_send, m2_recv,
    z_send, z_recv, x_send, x_recv, y_send, y_recv,
):
    rows = pb.shape[2]
    width = pb.shape[3]
    per_z = nx * ny
    dp = lax.axis_index("dp")
    sub = lax.axis_index("sub")
    z = dp // per_z
    xy = dp % per_z
    x = xy // ny
    y = xy % ny
    role = z % 4
    second = role // 2
    sign = 1 - 2 * second
    outer = (role % 3) == 0
    inner = jnp.logical_not(outer)

    def at_z(other):
        return (((other + 2 * NZ) % NZ) * per_z + xy, sub)

    up = at_z(z + sign)
    down = at_z(z - sign)
    twin = (dp, 1 - sub)

    def partner_z(level):
        step = 1 << level
        return z + step - 2 * step * ((z // step) % 2)

    partners = [at_z(partner_z(level)) for level in range(LEVELS)]
    far2 = at_z(z - 2 * sign)

    def remote(src, dst, send, recv, device):
        return pltpu.make_async_remote_copy(
            src_ref=src, dst_ref=dst, send_sem=send, recv_sem=recv,
            device_id=device, device_id_type=MESH,
        )

    def p_up(i, src, dst, k):
        return remote(pb.at[src, k], pb.at[dst, k], p_send_up.at[i, k], p_recv.at[dst, k], up)

    def p_dn(i, src, dst, k):
        return remote(pb.at[src, k], pb.at[dst, k], p_send_dn.at[i, k], p_recv.at[dst, k], down)

    def q_up(i, src, dst, k):
        return remote(qb.at[src, k], qb.at[dst, k], q_send_up.at[i, k], q_recv.at[dst, k], up)

    def q_dn(i, src, dst, k):
        return remote(qb.at[src, k], qb.at[dst, k], q_send_dn.at[i, k], q_recv.at[dst, k], down)

    def c_up(k):
        return remote(cs.at[k], cin.at[k], c_send.at[0, k], c_recv.at[k], up)

    def c_dn(k):
        return remote(cm.at[k], cin.at[k], c_send.at[1, k], c_recv.at[k], down)

    def p_wait(slot, k):
        remote(pb.at[slot, k], pb.at[slot, k], p_send_up.at[0, k], p_recv.at[slot, k], up).wait_recv()

    def q_wait(slot, k):
        remote(qb.at[slot, k], qb.at[slot, k], q_send_up.at[0, k], q_recv.at[slot, k], up).wait_recv()

    def tile_copy(i):
        return remote(part.at[i], got.at[i], t_send.at[i], t_recv.at[i], twin)

    def finish_tile(i):
        tile_copy(i).wait_recv()
        got[i] = (got[i] + part[i]) * scale

    def m1_copy(level):
        return remote(ms1.at[level], mr1.at[level], m1_send.at[level], m1_recv.at[level], partners[level])

    def m2_copy(i):
        device = partners[i] if i < LEVELS else far2
        return remote(ms2, mr2.at[i], m2_send.at[i], m2_recv.at[i], device)

    def z_copy(d):
        return remote(lz.at[z], lz.at[z], z_send.at[d], z_recv.at[z], at_z(z + d))

    def z_wait(d):
        other = (z + d) % NZ
        remote(lz.at[other], lz.at[other], z_send.at[d], z_recv.at[other], at_z(z + d)).wait_recv()

    def x_device(d):
        return (z * per_z + ((x + d) % nx) * ny + y, sub)

    def x_copy(d):
        return remote(lx.at[x], lx.at[x], x_send.at[d], x_recv.at[x], x_device(d))

    def x_wait(d):
        other = (x + d) % nx
        remote(lx.at[other], lx.at[other], x_send.at[d], x_recv.at[other], x_device(d)).wait_recv()

    def y_device(d):
        return (z * per_z + x * ny + (y + d) % ny, sub)

    def y_copy(d):
        return remote(ly.at[y], ly.at[y], y_send.at[d], y_recv.at[y], y_device(d))

    def y_wait(d):
        other = (y + d) % ny
        remote(ly.at[other], ly.at[other], y_send.at[d], y_recv.at[other], y_device(d)).wait_recv()

    def load_p(k):
        return pltpu.make_async_copy(
            p_hbm.at[:, pl.ds(pl.multiple_of(k * width, width), width)], pb.at[P_OWN, k], own_sem.at[0, k]
        )

    def load_q(k):
        return pltpu.make_async_copy(
            q_hbm.at[:, pl.ds(pl.multiple_of(k * width, width), width)], qb.at[Q_OWN, k], own_sem.at[1, k]
        )

    def store_dq(k):
        return pltpu.make_async_copy(
            dqv.at[k], dq_hbm.at[:, pl.ds(pl.multiple_of(k * width, width), width)], out_sem.at[0, k]
        )

    def store_dp(k):
        return pltpu.make_async_copy(
            dpv.at[k], dp_hbm.at[:, pl.ds(pl.multiple_of(k * width, width), width)], out_sem.at[1, k]
        )

    def each_chunk(body):
        def step(k, carry):
            body(k)
            return carry

        lax.fori_loop(0, CHUNKS, step, 0)

    def each_step(body):
        def step(k, carry):
            body(k)
            return carry

        lax.fori_loop(0, CHUNKS + LAG, step, 0)

    def add_tile(i, k, left, right):
        @pl.when(k == 0)
        def _():
            part[i] = dot_nt(left, right)

        @pl.when(k > 0)
        def _():
            part[i] = part[i] + dot_nt(left, right)

    @each_chunk
    def _(k):
        load_p(k).start()

    @each_chunk
    def _(k):
        load_q(k).start()

    barrier = pltpu.get_barrier_semaphore()
    greeted = [twin]
    greeted += [at_z(z + d) for d in range(1, NZ)]
    greeted += [x_device(d) for d in range(1, nx)]
    greeted += [y_device(d) for d in range(1, ny)]
    for device in greeted:
        pl.semaphore_signal(barrier, inc=1, device_id=device, device_id_type=MESH)
    pl.semaphore_wait(barrier, len(greeted))

    @each_chunk
    def _(k):
        load_p(k).wait()

        @pl.when(outer)
        def _():
            p_up(0, P_OWN, P_DN0, k).start()

        @pl.when(inner)
        def _():
            p_up(0, P_OWN, P_UP0, k).start()

            @pl.when(k < EARLY)
            def _():
                p_dn(0, P_OWN, P_UP0, k).start()

    @each_chunk
    def _(k):
        load_q(k).wait()

    near = jnp.where(outer, P_UP0, P_DN0)
    active = [pair_ref[level, dp] > 0 for level in range(LEVELS)]
    x_active = pair_ref[2, partner_z(1) * per_z + xy] > 0

    def add_up(level, slot, k):
        add_tile(T_U0 + level, k, qb[Q_OWN, k], pb[slot, k])

    def add_low(level, slot, k):
        add_tile(T_L0 + level, k, pb[P_OWN, k], qb[slot, k])

    def add_own(k):
        add_tile(T_OWN, k, pb[P_OWN, k], qb[Q_OWN, k])

    def up_stats(level):
        finish_tile(T_U0 + level)
        tile = got[T_U0 + level]
        ms1[level] = jnp.broadcast_to(lse_cols(tile), (8, rows))
        m1_copy(level).start()
        lse[2 + level:3 + level, :] = to_lanes(lse_rows(tile))

    def own_stats():
        finish_tile(T_OWN)
        lse[0:1, :] = lse_cols(got[T_OWN])
        lse[1:2, :] = to_lanes(lse_rows(got[T_OWN]))

    def gather(parts):
        parts = [parts[0]] + [jnp.where(a, v, -jnp.inf) for a, v in zip(active, parts[1:])]
        top = functools.reduce(jnp.maximum, parts)
        return top + jnp.log(functools.reduce(jnp.add, [jnp.exp(v - top) for v in parts]))

    def all_stats():
        for level in range(LEVELS):
            m1_copy(level).wait_recv()
        row_lse = gather([lse[0:1, :]] + [lse[2 + level:3 + level, :] for level in range(LEVELS)])
        col_lse = gather([lse[1:2, :]] + [mr1[level][0:1, :] for level in range(LEVELS)])
        lse[5:6, :] = row_lse
        lse[6:7, :] = col_lse
        ms2[0:4, :] = jnp.broadcast_to(row_lse, (4, rows))
        ms2[4:8, :] = jnp.broadcast_to(col_lse, (4, rows))
        for level in range(LEVELS):
            m2_copy(level).start()

    def hits():
        return (pos_ref[...] == lax.broadcasted_iota(jnp.int32, (rows, rows), 0)).astype(F32)

    def loss_start():
        share = jnp.sum(lse[5:7, :]) - 2.0 * jnp.sum(got[T_OWN] * hits())
        lz[z] = jnp.full((8, 128), share, F32)
        for d in range(1, NZ):
            z_copy(d).start()

    def loss_x():
        for d in range(1, NZ):
            z_wait(d)
        lx[x] = functools.reduce(jnp.add, [lz[i] for i in range(NZ)])
        for d in range(1, nx):
            x_copy(d).start()

    def loss_y():
        for d in range(1, nx):
            x_wait(d)
        ly[y] = functools.reduce(jnp.add, [lx[i] for i in range(nx)])
        for d in range(1, ny):
            y_copy(d).start()

    def own_grads():
        tile = got[T_OWN]
        grad = jnp.exp(tile - lse[5:6, :]) + jnp.exp(tile - to_column(lse[6:7, :])) - 2.0 * hits()
        g_own_t[...] = grad.astype(BF16)
        g_own[...] = jnp.transpose(grad).astype(BF16)

    def up_grad(level, also_t=False):
        tile = got[T_U0 + level]
        grad = jnp.exp(tile - to_column(lse[5:6, :])) + jnp.exp(tile - mr2[level][4:5, :])
        grad = jnp.where(active[level], grad, 0.0)
        g_up[level] = grad.astype(BF16)
        if also_t:
            g_up0_t[...] = jnp.transpose(grad).astype(BF16)

    def low_grad(level):
        finish_tile(T_L0 + level)
        tile = got[T_L0 + level]
        grad = jnp.exp(tile - mr2[level][0:1, :]) + jnp.exp(tile - to_column(lse[6:7, :]))
        g_low[level] = jnp.where(active[level], grad, 0.0).astype(BF16)

    def c_wait(k):
        remote(cs.at[k], cin.at[k], c_send.at[0, k], c_recv.at[k], up).wait_recv()

    def query_grad(k):
        total = dot_nn(g_own[...], pb[P_OWN, k])
        total = total + dot_nn(g_up[0], pb[near, k])
        total = total + dot_nn(g_up[1], pb[P_UP1, k])
        dqv[k] = total + dot_nn(g_up[2], pb[P_DN1, k])
        store_dq(k).start()

    def add_passage_grad(level, slot):
        @each_chunk
        def _(k):
            dpv[k] = dpv[k] + dot_nn(g_low[level], qb[slot, k])

    def q_far(k):
        q_wait(Q_DN2, k)
        q_up(0, Q_DN2, Q_DN2, k).start()

    def at(k, step, body):
        pl.when(k == step)(body)

    @pl.when(outer)
    def _():
        for k in range(EARLY):
            q_dn(0, Q_OWN, Q_DN2, k).start()

        @each_step
        def _(k):
            @pl.when(k < CHUNKS)
            def _():
                p_wait(P_UP1, k)
                p_dn(0, P_UP1, P_DN0, k).start()
                add_up(1, P_UP1, k)

            @pl.when(k >= LAG)
            def _():
                p_wait(P_DN0, k - LAG)
                p_up(1, P_DN0, P_DN1, k - LAG).start()

        tile_copy(T_U0 + 1).start()
        for k in range(NEAR):
            q_up(1, Q_OWN, Q_DN0, k).start()
        for k in range(EARLY):
            q_far(k)

        @each_step
        def _(k):
            @pl.when(k < CHUNKS)
            def _():
                p_wait(P_UP2, k)
                p_dn(1, P_UP2, P_DN1, k).start()
                add_own(k)

            @pl.when(k >= LAG)
            def _():
                p_wait(P_DN1, k - LAG)
                add_up(2, P_DN1, k - LAG)

            at(k, 2, lambda: up_stats(1))

            @pl.when(k == CHUNKS - 1)
            def _():
                for j in range(EARLY, CHUNKS):
                    q_dn(0, Q_OWN, Q_DN2, j).start()

        tile_copy(T_OWN).start()
        tile_copy(T_U0 + 2).start()
        own_stats()
        up_stats(2)

        @each_chunk
        def _(k):
            p_wait(P_UP0, k)
            add_up(0, P_UP0, k)

            @pl.when(k >= EARLY + LAG)
            def _():
                q_far(k - LAG)

        tile_copy(T_U0).start()
        up_stats(0)
        q_far(CHUNKS - LAG)
        all_stats()
        m2_copy(LEVELS).start()
        for k in range(CHUNKS - LAG + 1, CHUNKS):
            q_far(k)
        for k in range(NEAR, CHUNKS):
            q_up(1, Q_OWN, Q_DN0, k).start()

        @each_step
        def _(k):
            @pl.when(k < CHUNKS)
            def _():
                q_wait(Q_UP1, k)
                q_dn(1, Q_UP1, Q_DN0, k).start()
                add_low(1, Q_UP1, k)

            @pl.when(k >= LAG)
            def _():
                q_wait(Q_DN0, k - LAG)
                q_up(2, Q_DN0, Q_DN1, k - LAG).start()

            at(k, 2, loss_start)
            at(k, 3, own_grads)

        tile_copy(T_L0 + 1).start()
        for level in range(LEVELS):
            m2_copy(level).wait_recv()
            up_grad(level)
        low_grad(1)
        loss_x()

        @each_chunk
        def _(k):
            query_grad(k)
            dpv[k] = dot_nn(g_own_t[...], qb[Q_OWN, k]) + dot_nn(g_low[1], qb[Q_UP1, k])

        loss_y()

        @each_chunk
        def _(k):
            c_wait(k)
            dpv[k] = dpv[k] + cin[k].astype(F32)
            store_dp(k).start()

    @pl.when(inner)
    def _():
        @each_chunk
        def _(k):
            p_wait(P_UP0, k)
            p_dn(1, P_UP0, P_UP1, k).start()
            p_wait(P_DN0, k)
            p_up(1, P_DN0, P_UP1, k).start()
            add_up(0, P_DN0, k)

        tile_copy(T_U0).start()

        @each_chunk
        def _(k):
            q_up(0, Q_OWN, Q_UP0, k).start()

        @each_chunk
        def _(k):
            p_wait(P_UP1, k)
            p_dn(2, P_UP1, P_UP2, k).start()
            add_up(1, P_UP1, k)

        for k in range(EARLY, CHUNKS):
            p_dn(0, P_OWN, P_UP0, k).start()
        tile_copy(T_U0 + 1).start()

        @each_chunk
        def _(k):
            add_own(k)
            p_wait(P_DN1, k)
            add_up(2, P_DN1, k)

        tile_copy(T_OWN).start()
        tile_copy(T_U0 + 2).start()
        up_stats(0)
        up_stats(1)
        up_stats(2)
        own_stats()

        @each_chunk
        def _(k):
            q_wait(Q_UP0, k)
            q_dn(0, Q_UP0, Q_UP1, k).start()

            @pl.when(k < NEAR)
            def _():
                q_wait(Q_DN0, k)
                q_up(1, Q_DN0, Q_UP1, k).start()
                add_low(0, Q_DN0, k)

        def add_x(k):
            q_wait(Q_DN2, k)
            add_tile(T_X, k, pb[P_UP1, k], qb[Q_DN2, k])

        @each_chunk
        def _(k):
            add_x(k)
            at(k, CHUNKS - 2, all_stats)

        tile_copy(T_X).start()
        loss_start()
        finish_tile(T_X)
        m2_copy(1).wait_recv()
        m2_copy(LEVELS).wait_recv()
        tile = got[T_X]
        grad = jnp.exp(tile - mr2[LEVELS][0:1, :]) + jnp.exp(tile - to_column(mr2[1][4:5, :]))
        g_x[...] = jnp.where(x_active, grad, 0.0).astype(BF16)

        @each_chunk
        def _(k):
            cs[k] = dot_nn(g_x[...], qb[Q_DN2, k]).astype(BF16)
            c_up(k).start()

        m2_copy(0).wait_recv()
        up_grad(0, True)
        up_grad(1)
        m2_copy(2).wait_recv()
        up_grad(2)
        own_grads()

        @each_step
        def _(k):
            @pl.when(k < CHUNKS)
            def _():
                c_wait(k)
                cm[k] = (cin[k].astype(F32) + dot_nn(g_up0_t[...], qb[Q_OWN, k])).astype(BF16)
                c_dn(k).start()

            @pl.when(jnp.logical_and(k >= 1, k < 1 + CHUNKS - NEAR))
            def _():
                late = NEAR + k - 1
                q_wait(Q_DN0, late)
                q_up(1, Q_DN0, Q_UP1, late).start()
                add_low(0, Q_DN0, late)

            @pl.when(k < CHUNKS)
            def _():
                query_grad(k)
                dpv[k] = dot_nn(g_own_t[...], qb[Q_OWN, k])

            @pl.when(jnp.logical_and(k >= 2, k < 2 + NEAR))
            def _():
                q_wait(Q_UP1, k - 2)
                add_low(1, Q_UP1, k - 2)

            at(k, CHUNKS - NEAR + 1, lambda: tile_copy(T_L0).start())
            at(k, CHUNKS - NEAR + 2, lambda: low_grad(0))

        loss_x()

        @each_chunk
        def _(k):
            q_wait(Q_DN1, k)
            add_low(2, Q_DN1, k)

        tile_copy(T_L0 + 2).start()
        add_passage_grad(0, Q_DN0)
        low_grad(2)
        loss_y()
        add_passage_grad(2, Q_DN1)

        def rest(k, carry):
            q_wait(Q_UP1, k)
            add_low(1, Q_UP1, k)
            return carry

        lax.fori_loop(NEAR, CHUNKS, rest, 0)
        tile_copy(T_L0 + 1).start()
        low_grad(1)

        @each_chunk
        def _(k):
            dpv[k] = dpv[k] + dot_nn(g_low[1], qb[Q_UP1, k])
            store_dp(k).start()

    for d in range(1, ny):
        y_wait(d)
    total_loss = functools.reduce(jnp.add, [ly[i] for i in range(ny)])
    loss_ref[0] = jnp.max(total_loss) / count

    @each_chunk
    def _(k):
        store_dq(k).wait()
        store_dp(k).wait()
        p_up(0, P_OWN, P_DN0, k).wait_send()
        p_up(1, P_DN0, P_DN1, k).wait_send()
        p_dn(0, P_UP1, P_DN0, k).wait_send()
        p_dn(1, P_UP2, P_DN1, k).wait_send()
        q_up(0, Q_DN2, Q_DN2, k).wait_send()
        q_up(1, Q_OWN, Q_DN0, k).wait_send()
        q_dn(0, Q_OWN, Q_DN2, k).wait_send()

        @pl.when(outer)
        def _():
            q_up(2, Q_DN0, Q_DN1, k).wait_send()
            q_dn(1, Q_UP1, Q_DN0, k).wait_send()

        @pl.when(inner)
        def _():
            p_dn(2, P_UP1, P_UP2, k).wait_send()
            c_up(k).wait_send()
            c_dn(k).wait_send()

    tile_copy(T_OWN).wait_send()
    for level in range(LEVELS):
        tile_copy(T_U0 + level).wait_send()
        m1_copy(level).wait_send()
        m2_copy(level).wait_send()
    tile_copy(T_L0 + 1).wait_send()

    @pl.when(outer)
    def _():
        m2_copy(LEVELS).wait_send()

    @pl.when(inner)
    def _():
        tile_copy(T_X).wait_send()
        tile_copy(T_L0).wait_send()
        tile_copy(T_L0 + 2).wait_send()

    for d in range(1, NZ):
        z_copy(d).wait_send()
    for d in range(1, nx):
        x_copy(d).wait_send()
    for d in range(1, ny):
        y_copy(d).wait_send()


def local(nx, ny, queries, passages, positive, pair_on):
    rows, depth = queries.shape
    width = depth // CHUNKS
    full = depth * lax.axis_size("sub")
    count = 2.0 * rows * lax.axis_size("dp")
    dma = pltpu.SemaphoreType.DMA
    block = (CHUNKS, rows, width)
    tile = (rows, rows)
    anywhere = pl.BlockSpec(memory_space=pl.ANY)
    return pl.pallas_call(
        functools.partial(kernel, nx, ny, 1.0 / math.sqrt(full), count),
        out_shape=(
            jax.ShapeDtypeStruct((1,), F32),
            jax.ShapeDtypeStruct((rows, depth), F32),
            jax.ShapeDtypeStruct((rows, depth), F32),
        ),
        in_specs=[
            anywhere,
            anywhere,
            pl.BlockSpec(memory_space=pltpu.VMEM),
            pl.BlockSpec(memory_space=pltpu.SMEM),
        ],
        out_specs=(pl.BlockSpec(memory_space=pltpu.SMEM), anywhere, anywhere),
        scratch_shapes=[
            pltpu.VMEM((6,) + block, BF16),
            pltpu.VMEM((6,) + block, BF16),
            pltpu.VMEM(block, BF16),
            pltpu.VMEM(block, BF16),
            pltpu.VMEM(block, BF16),
            pltpu.VMEM((8,) + tile, F32),
            pltpu.VMEM((8,) + tile, F32),
            pltpu.VMEM(block, F32),
            pltpu.VMEM(block, F32),
            pltpu.VMEM(tile, BF16),
            pltpu.VMEM(tile, BF16),
            pltpu.VMEM((LEVELS,) + tile, BF16),
            pltpu.VMEM(tile, BF16),
            pltpu.VMEM((LEVELS,) + tile, BF16),
            pltpu.VMEM(tile, BF16),
            pltpu.VMEM((8, rows), F32),
            pltpu.VMEM((LEVELS, 8, rows), F32),
            pltpu.VMEM((LEVELS, 8, rows), F32),
            pltpu.VMEM((8, rows), F32),
            pltpu.VMEM((LEVELS + 1, 8, rows), F32),
            pltpu.VMEM((NZ, 8, 128), F32),
            pltpu.VMEM((nx, 8, 128), F32),
            pltpu.VMEM((ny, 8, 128), F32),
            dma((2, CHUNKS)),
            dma((2, CHUNKS)),
            dma((2, CHUNKS)),
            dma((3, CHUNKS)),
            dma((5, CHUNKS)),
            dma((3, CHUNKS)),
            dma((2, CHUNKS)),
            dma((5, CHUNKS)),
            dma((2, CHUNKS)),
            dma((CHUNKS,)),
            dma((8,)),
            dma((8,)),
            dma((LEVELS,)),
            dma((LEVELS,)),
            dma((LEVELS + 1,)),
            dma((LEVELS + 1,)),
            dma((NZ,)),
            dma((NZ,)),
            dma((nx,)),
            dma((nx,)),
            dma((ny,)),
            dma((ny,)),
        ],
        compiler_params=pltpu.CompilerParams(
            collective_id=1, has_side_effects=True, vmem_limit_bytes=58 << 20
        ),
        name="infonce",
    )(queries, passages, positive, jnp.transpose(pair_on))


def solution(mesh):
    per_z = mesh.shape["dp"] // NZ
    nx = math.isqrt(per_z)
    ny = per_z // nx
    return jax.shard_map(
        functools.partial(local, nx, ny),
        mesh=mesh,
        in_specs=(P("dp", "sub"), P("dp", "sub"), P("dp", None), P()),
        out_specs=(P(), P("dp", "sub"), P("dp", "sub")),
        check_vma=False,
    )
```

```python
import functools
import math

import jax
import jax.numpy as jnp
from jax import lax
from jax.experimental import pallas as pl
from jax.experimental.pallas import tpu as pltpu
from jax.sharding import PartitionSpec as P

MESH = pl.DeviceIdType.MESH
NZ = 8
LEVELS = 3
CHUNKS = 8
LAG = 2
SLOW = 3
EARLY = 2
FIRST = 3
NEAR = 4
F32 = jnp.float32
BF16 = jnp.bfloat16

P_UP0, P_UP1, P_UP2, P_DN0, P_DN1, P_OWN = range(6)
Q_UP0, Q_UP1, Q_DN0, Q_DN1, Q_DN2, Q_OWN = range(6)
T_OWN, T_U0, T_L0, T_X = 0, 1, 4, 7


def dot_nt(a, b):
    return lax.dot_general(a, b, (((1,), (1,)), ((), ())), preferred_element_type=F32)


def dot_nn(a, b):
    return jnp.dot(a, b, preferred_element_type=F32)


def to_lanes(column):
    rows = column.shape[0]
    return jnp.transpose(jnp.broadcast_to(column, (rows, 128)))[0:1, :]


def to_column(lanes):
    rows = lanes.shape[1]
    return jnp.transpose(jnp.broadcast_to(lanes, (128, rows)))[:, 0:1]


def lse_rows(tile):
    top = jnp.max(tile, axis=1, keepdims=True)
    return top + jnp.log(jnp.sum(jnp.exp(tile - top), axis=1, keepdims=True))


def lse_cols(tile):
    top = jnp.max(tile, axis=0, keepdims=True)
    return top + jnp.log(jnp.sum(jnp.exp(tile - top), axis=0, keepdims=True))


def kernel(
    nx, ny, scale, count,
    q_hbm, p_hbm, pos_ref, pair_ref,
    loss_ref, dq_hbm, dp_hbm, block_hbm, grad_hbm,
    pb, qb, cin, cs, cm, part, got, dqv, dpv,
    g_own, g_own_t, g_up, g_up0_t, g_low, g_x, lse,
    ms1, mr1, ms2, mr2, lz, lx, ly,
    own_sem, out_sem, last_sem,
    p_send_up, p_send_dn, p_recv,
    q_send_up, q_send_dn, q_recv,
    c_send, c_recv,
    t_send, t_recv,
    m1_send, m1_recv, m2_send, m2_recv,
    z_send, z_recv, x_send, x_recv, y_send, y_recv,
):
    rows = pb.shape[2]
    width = pb.shape[3]
    per_z = nx * ny
    dp = lax.axis_index("dp")
    sub = lax.axis_index("sub")
    z = dp // per_z
    xy = dp % per_z
    x = xy // ny
    y = xy % ny
    role = z % 4
    second = role // 2
    sign = 1 - 2 * second
    outer = (role % 3) == 0
    inner = jnp.logical_not(outer)

    def at_z(other):
        return (((other + 2 * NZ) % NZ) * per_z + xy, sub)

    up = at_z(z + sign)
    down = at_z(z - sign)
    twin = (dp, 1 - sub)

    def partner_z(level):
        step = 1 << level
        return z + step - 2 * step * ((z // step) % 2)

    partners = [at_z(partner_z(level)) for level in range(LEVELS)]
    far2 = at_z(z - 2 * sign)

    def remote(src, dst, send, recv, device):
        return pltpu.make_async_remote_copy(
            src_ref=src, dst_ref=dst, send_sem=send, recv_sem=recv,
            device_id=device, device_id_type=MESH,
        )

    def p_up(i, src, dst, k):
        return remote(pb.at[src, k], pb.at[dst, k], p_send_up.at[i, k], p_recv.at[dst, k], up)

    def p_dn(i, src, dst, k):
        return remote(pb.at[src, k], pb.at[dst, k], p_send_dn.at[i, k], p_recv.at[dst, k], down)

    def q_up(i, src, dst, k):
        return remote(qb.at[src, k], qb.at[dst, k], q_send_up.at[i, k], q_recv.at[dst, k], up)

    def q_dn(i, src, dst, k):
        return remote(qb.at[src, k], qb.at[dst, k], q_send_dn.at[i, k], q_recv.at[dst, k], down)

    def c_up(k):
        return remote(cs.at[k], cin.at[k], c_send.at[0, k], c_recv.at[k], up)

    def c_dn(k):
        return remote(cm.at[k], cin.at[k], c_send.at[1, k], c_recv.at[k], down)

    def p_wait(slot, k):
        remote(pb.at[slot, k], pb.at[slot, k], p_send_up.at[0, k], p_recv.at[slot, k], up).wait_recv()

    def q_wait(slot, k):
        remote(qb.at[slot, k], qb.at[slot, k], q_send_up.at[0, k], q_recv.at[slot, k], up).wait_recv()

    def tile_copy(i):
        return remote(part.at[i], got.at[i], t_send.at[i], t_recv.at[i], twin)

    def finish_tile(i):
        tile_copy(i).wait_recv()
        got[i] = (got[i] + part[i]) * scale

    def m1_copy(level):
        return remote(ms1.at[level], mr1.at[level], m1_send.at[level], m1_recv.at[level], partners[level])

    def m2_copy(i):
        device = partners[i] if i < LEVELS else far2
        return remote(ms2, mr2.at[i], m2_send.at[i], m2_recv.at[i], device)

    def z_copy(d):
        return remote(lz.at[z], lz.at[z], z_send.at[d], z_recv.at[z], at_z(z + d))

    def z_wait(d):
        other = (z + d) % NZ
        remote(lz.at[other], lz.at[other], z_send.at[d], z_recv.at[other], at_z(z + d)).wait_recv()

    def x_device(d):
        return (z * per_z + ((x + d) % nx) * ny + y, sub)

    def x_copy(d):
        return remote(lx.at[x], lx.at[x], x_send.at[d], x_recv.at[x], x_device(d))

    def x_wait(d):
        other = (x + d) % nx
        remote(lx.at[other], lx.at[other], x_send.at[d], x_recv.at[other], x_device(d)).wait_recv()

    def y_device(d):
        return (z * per_z + x * ny + (y + d) % ny, sub)

    def y_copy(d):
        return remote(ly.at[y], ly.at[y], y_send.at[d], y_recv.at[y], y_device(d))

    def y_wait(d):
        other = (y + d) % ny
        remote(ly.at[other], ly.at[other], y_send.at[d], y_recv.at[other], y_device(d)).wait_recv()

    def load_p(k):
        return pltpu.make_async_copy(
            p_hbm.at[:, pl.ds(pl.multiple_of(k * width, width), width)], pb.at[P_OWN, k], own_sem.at[0, k]
        )

    def load_q(k):
        return pltpu.make_async_copy(
            q_hbm.at[:, pl.ds(pl.multiple_of(k * width, width), width)], qb.at[Q_OWN, k], own_sem.at[1, k]
        )

    def store_dq(k):
        return pltpu.make_async_copy(
            dqv.at[k], dq_hbm.at[:, pl.ds(pl.multiple_of(k * width, width), width)], out_sem.at[0, k]
        )

    def store_dp(k):
        return pltpu.make_async_copy(
            dpv.at[k], dp_hbm.at[:, pl.ds(pl.multiple_of(k * width, width), width)], out_sem.at[1, k]
        )

    def store_block(k):
        @pl.when(outer)
        def _():
            pltpu.make_async_copy(cin.at[k], block_hbm.at[k], last_sem.at[k]).start()

        @pl.when(inner)
        def _():
            pltpu.make_async_copy(qb.at[Q_UP1, k], block_hbm.at[k], last_sem.at[k]).start()

    def store_grad(i):
        return pltpu.make_async_copy(g_low.at[i], grad_hbm, last_sem.at[CHUNKS])

    def each_chunk(body):
        def step(k, carry):
            body(k)
            return carry

        lax.fori_loop(0, CHUNKS, step, 0)

    def each_step(body):
        def step(k, carry):
            body(k)
            return carry

        lax.fori_loop(0, CHUNKS + LAG, step, 0)

    def add_tile(i, k, left, right):
        @pl.when(k == 0)
        def _():
            part[i] = dot_nt(left, right)

        @pl.when(k > 0)
        def _():
            part[i] = part[i] + dot_nt(left, right)

    @each_chunk
    def _(k):
        load_p(k).start()

    @each_chunk
    def _(k):
        load_q(k).start()

    barrier = pltpu.get_barrier_semaphore()
    greeted = [twin]
    greeted += [at_z(z + d) for d in range(1, NZ)]
    greeted += [x_device(d) for d in range(1, nx)]
    greeted += [y_device(d) for d in range(1, ny)]
    for device in greeted:
        pl.semaphore_signal(barrier, inc=1, device_id=device, device_id_type=MESH)
    pl.semaphore_wait(barrier, len(greeted))

    @each_chunk
    def _(k):
        load_p(k).wait()

        @pl.when(outer)
        def _():
            p_up(0, P_OWN, P_DN0, k).start()

        @pl.when(inner)
        def _():
            p_up(0, P_OWN, P_UP0, k).start()

            @pl.when(k < EARLY)
            def _():
                p_dn(0, P_OWN, P_UP0, k).start()

    @each_chunk
    def _(k):
        load_q(k).wait()

    near = jnp.where(outer, P_UP0, P_DN0)
    active = [pair_ref[level, dp] > 0 for level in range(LEVELS)]
    x_active = pair_ref[2, partner_z(1) * per_z + xy] > 0

    def add_up(level, slot, k):
        add_tile(T_U0 + level, k, qb[Q_OWN, k], pb[slot, k])

    def add_low(level, slot, k):
        add_tile(T_L0 + level, k, pb[P_OWN, k], qb[slot, k])

    def add_own(k):
        add_tile(T_OWN, k, pb[P_OWN, k], qb[Q_OWN, k])

    def up_stats(level):
        finish_tile(T_U0 + level)
        tile = got[T_U0 + level]
        ms1[level] = jnp.broadcast_to(lse_cols(tile), (8, rows))
        m1_copy(level).start()
        lse[2 + level:3 + level, :] = to_lanes(lse_rows(tile))

    def own_stats():
        finish_tile(T_OWN)
        lse[0:1, :] = lse_cols(got[T_OWN])
        lse[1:2, :] = to_lanes(lse_rows(got[T_OWN]))

    def gather(parts):
        parts = [parts[0]] + [jnp.where(a, v, -jnp.inf) for a, v in zip(active, parts[1:])]
        top = functools.reduce(jnp.maximum, parts)
        return top + jnp.log(functools.reduce(jnp.add, [jnp.exp(v - top) for v in parts]))

    def all_stats():
        for level in range(LEVELS):
            m1_copy(level).wait_recv()
        row_lse = gather([lse[0:1, :]] + [lse[2 + level:3 + level, :] for level in range(LEVELS)])
        col_lse = gather([lse[1:2, :]] + [mr1[level][0:1, :] for level in range(LEVELS)])
        lse[5:6, :] = row_lse
        lse[6:7, :] = col_lse
        ms2[0:4, :] = jnp.broadcast_to(row_lse, (4, rows))
        ms2[4:8, :] = jnp.broadcast_to(col_lse, (4, rows))
        for level in range(LEVELS):
            m2_copy(level).start()

    def hits():
        return (pos_ref[...] == lax.broadcasted_iota(jnp.int32, (rows, rows), 0)).astype(F32)

    def loss_start():
        share = jnp.sum(lse[5:7, :]) - 2.0 * jnp.sum(got[T_OWN] * hits())
        lz[z] = jnp.full((8, 128), share, F32)
        for d in range(1, NZ):
            z_copy(d).start()

    def loss_x():
        for d in range(1, NZ):
            z_wait(d)
        lx[x] = functools.reduce(jnp.add, [lz[i] for i in range(NZ)])
        for d in range(1, nx):
            x_copy(d).start()

    def loss_y():
        for d in range(1, nx):
            x_wait(d)
        ly[y] = functools.reduce(jnp.add, [lx[i] for i in range(nx)])
        for d in range(1, ny):
            y_copy(d).start()

    def own_grads():
        tile = got[T_OWN]
        grad = jnp.exp(tile - lse[5:6, :]) + jnp.exp(tile - to_column(lse[6:7, :])) - 2.0 * hits()
        g_own_t[...] = grad.astype(BF16)
        g_own[...] = jnp.transpose(grad).astype(BF16)

    def up_grad(level, also_t=False):
        tile = got[T_U0 + level]
        grad = jnp.exp(tile - to_column(lse[5:6, :])) + jnp.exp(tile - mr2[level][4:5, :])
        grad = jnp.where(active[level], grad, 0.0)
        g_up[level] = grad.astype(BF16)
        if also_t:
            g_up0_t[...] = jnp.transpose(grad).astype(BF16)

    def low_grad(level):
        finish_tile(T_L0 + level)
        tile = got[T_L0 + level]
        grad = jnp.exp(tile - mr2[level][0:1, :]) + jnp.exp(tile - to_column(lse[6:7, :]))
        g_low[level] = jnp.where(active[level], grad, 0.0).astype(BF16)

    def c_wait(k):
        remote(cs.at[k], cin.at[k], c_send.at[0, k], c_recv.at[k], up).wait_recv()

    def settle():
        @each_chunk
        def _(k):
            store_dq(k).wait()
            p_up(0, P_OWN, P_DN0, k).wait_send()
            p_up(1, P_DN0, P_DN1, k).wait_send()
            p_dn(0, P_UP1, P_DN0, k).wait_send()
            p_dn(1, P_UP2, P_DN1, k).wait_send()
            q_up(0, Q_DN2, Q_DN2, k).wait_send()
            q_dn(0, Q_OWN, Q_DN2, k).wait_send()

        tile_copy(T_OWN).wait_send()
        for level in range(LEVELS):
            tile_copy(T_U0 + level).wait_send()
            m1_copy(level).wait_send()
            m2_copy(level).wait_send()
        for d in range(1, NZ):
            z_copy(d).wait_send()

    def loss_end():
        for d in range(1, ny):
            y_wait(d)
        total_loss = functools.reduce(jnp.add, [ly[i] for i in range(ny)])
        loss_ref[0] = jnp.max(total_loss) / count
        for d in range(1, nx):
            x_copy(d).wait_send()
        for d in range(1, ny):
            y_copy(d).wait_send()

    def query_grad(k):
        total = dot_nn(g_own[...], pb[P_OWN, k])
        total = total + dot_nn(g_up[0], pb[near, k])
        total = total + dot_nn(g_up[1], pb[P_UP1, k])
        dqv[k] = total + dot_nn(g_up[2], pb[P_DN1, k])
        store_dq(k).start()

    def q_far(k):
        q_wait(Q_DN2, k)
        q_up(0, Q_DN2, Q_DN2, k).start()

    def at(k, step, body):
        pl.when(k == step)(body)

    @pl.when(outer)
    def _():
        for k in range(FIRST):
            q_dn(0, Q_OWN, Q_DN2, k).start()

        @each_step
        def _(k):
            @pl.when(k < CHUNKS)
            def _():
                p_wait(P_UP1, k)
                p_dn(0, P_UP1, P_DN0, k).start()
                add_up(1, P_UP1, k)

            @pl.when(k >= LAG)
            def _():
                p_wait(P_DN0, k - LAG)
                p_up(1, P_DN0, P_DN1, k - LAG).start()

        tile_copy(T_U0 + 1).start()
        for k in range(NEAR):
            q_up(1, Q_OWN, Q_DN0, k).start()
        for k in range(EARLY):
            q_far(k)

        @each_step
        def _(k):
            @pl.when(k < CHUNKS)
            def _():
                p_wait(P_UP2, k)
                p_dn(1, P_UP2, P_DN1, k).start()
                add_own(k)

            @pl.when(k >= LAG)
            def _():
                p_wait(P_DN1, k - LAG)
                add_up(2, P_DN1, k - LAG)

            at(k, 2, lambda: up_stats(1))

            @pl.when(k == CHUNKS - 1)
            def _():
                for j in range(FIRST, CHUNKS):
                    q_dn(0, Q_OWN, Q_DN2, j).start()

        tile_copy(T_OWN).start()
        tile_copy(T_U0 + 2).start()
        own_stats()
        up_stats(2)

        @each_chunk
        def _(k):
            p_wait(P_UP0, k)
            add_up(0, P_UP0, k)

            @pl.when(k >= EARLY + LAG)
            def _():
                q_far(k - LAG)

        tile_copy(T_U0).start()
        up_stats(0)
        q_far(CHUNKS - LAG)
        all_stats()
        m2_copy(LEVELS).start()
        for k in range(CHUNKS - LAG + 1, CHUNKS):
            q_far(k)
        for k in range(NEAR, CHUNKS):
            q_up(1, Q_OWN, Q_DN0, k).start()

        @each_step
        def _(k):
            @pl.when(k < CHUNKS)
            def _():
                q_wait(Q_UP1, k)
                q_dn(1, Q_UP1, Q_DN0, k).start()
                add_low(1, Q_UP1, k)

            @pl.when(k >= LAG)
            def _():
                q_wait(Q_DN0, k - LAG)
                q_up(2, Q_DN0, Q_DN1, k - LAG).start()

            at(k, 2, loss_start)
            at(k, 3, own_grads)

        tile_copy(T_L0 + 1).start()
        for level in range(LEVELS):
            m2_copy(level).wait_recv()
            up_grad(level)
        low_grad(1)
        loss_x()

        @each_chunk
        def _(k):
            query_grad(k)
            dpv[k] = dot_nn(g_own_t[...], qb[Q_OWN, k]) + dot_nn(g_low[1], qb[Q_UP1, k])
            store_dp(k).start()

        i = lax.broadcasted_iota(jnp.int32, (rows, rows), 0)
        j = lax.broadcasted_iota(jnp.int32, (rows, rows), 1)
        g_low[0] = (i == j).astype(F32).astype(BF16)
        store_grad(0).start()
        loss_y()
        settle()
        loss_end()
        m2_copy(LEVELS).wait_send()

        @each_chunk
        def _(k):
            q_dn(1, Q_UP1, Q_DN0, k).wait_send()

        @each_chunk
        def _(k):
            c_wait(k)
            store_block(k)

    @pl.when(inner)
    def _():
        @each_chunk
        def _(k):
            p_wait(P_UP0, k)
            p_dn(1, P_UP0, P_UP1, k).start()
            p_wait(P_DN0, k)
            p_up(1, P_DN0, P_UP1, k).start()
            add_up(0, P_DN0, k)

        tile_copy(T_U0).start()

        @each_chunk
        def _(k):
            q_up(0, Q_OWN, Q_UP0, k).start()

        @each_chunk
        def _(k):
            p_wait(P_UP1, k)
            p_dn(2, P_UP1, P_UP2, k).start()
            add_up(1, P_UP1, k)

        for k in range(EARLY, CHUNKS):
            p_dn(0, P_OWN, P_UP0, k).start()
        tile_copy(T_U0 + 1).start()

        @each_chunk
        def _(k):
            add_own(k)
            p_wait(P_DN1, k)
            add_up(2, P_DN1, k)

        tile_copy(T_OWN).start()
        tile_copy(T_U0 + 2).start()
        up_stats(0)
        up_stats(1)
        up_stats(2)
        own_stats()

        @each_chunk
        def _(k):
            q_wait(Q_UP0, k)
            q_dn(0, Q_UP0, Q_UP1, k).start()

            @pl.when(k < NEAR)
            def _():
                q_wait(Q_DN0, k)
                q_up(1, Q_DN0, Q_UP1, k).start()
                add_low(0, Q_DN0, k)

        def add_x(k):
            q_wait(Q_DN2, k)
            add_tile(T_X, k, pb[P_UP1, k], qb[Q_DN2, k])

        @each_chunk
        def _(k):
            add_x(k)
            at(k, CHUNKS - 2, all_stats)

        tile_copy(T_X).start()
        loss_start()
        finish_tile(T_X)
        m2_copy(1).wait_recv()
        m2_copy(LEVELS).wait_recv()
        tile = got[T_X]
        grad = jnp.exp(tile - mr2[LEVELS][0:1, :]) + jnp.exp(tile - to_column(mr2[1][4:5, :]))
        g_x[...] = jnp.where(x_active, grad, 0.0).astype(BF16)

        @each_chunk
        def _(k):
            cs[k] = dot_nn(g_x[...], qb[Q_DN2, k]).astype(BF16)
            c_up(k).start()

        m2_copy(0).wait_recv()
        up_grad(0, True)
        up_grad(1)
        m2_copy(2).wait_recv()
        up_grad(2)
        own_grads()

        @each_step
        def _(k):
            @pl.when(k < CHUNKS)
            def _():
                c_wait(k)
                cm[k] = (cin[k].astype(F32) + dot_nn(g_up0_t[...], qb[Q_OWN, k])).astype(BF16)
                c_dn(k).start()

            @pl.when(jnp.logical_and(k >= 1, k < 1 + CHUNKS - NEAR))
            def _():
                late = NEAR + k - 1
                q_wait(Q_DN0, late)
                q_up(1, Q_DN0, Q_UP1, late).start()
                add_low(0, Q_DN0, late)

            @pl.when(k < CHUNKS)
            def _():
                query_grad(k)
                dpv[k] = dot_nn(g_own_t[...], qb[Q_OWN, k])

            @pl.when(jnp.logical_and(k >= 2, k < 2 + NEAR))
            def _():
                q_wait(Q_UP1, k - 2)
                store_block(k - 2)
                add_low(1, Q_UP1, k - 2)

            at(k, CHUNKS - NEAR + 1, lambda: tile_copy(T_L0).start())
            at(k, CHUNKS - NEAR + 2, lambda: low_grad(0))

            @pl.when(k >= SLOW)
            def _():
                q_wait(Q_DN1, k - SLOW)
                add_low(2, Q_DN1, k - SLOW)

        @each_chunk
        def _(k):
            dpv[k] = dpv[k] + dot_nn(g_low[0], qb[Q_DN0, k])

        loss_x()

        def rest_of_dn1(k, carry):
            q_wait(Q_DN1, k)
            add_low(2, Q_DN1, k)
            return carry

        lax.fori_loop(CHUNKS + LAG - SLOW, CHUNKS, rest_of_dn1, 0)
        tile_copy(T_L0 + 2).start()
        settle()

        @each_chunk
        def _(k):
            p_dn(2, P_UP1, P_UP2, k).wait_send()
            c_up(k).wait_send()

        def rest_of_up1(k, carry):
            q_wait(Q_UP1, k)
            store_block(k)
            add_low(1, Q_UP1, k)
            return carry

        lax.fori_loop(NEAR, CHUNKS - 2, rest_of_up1, 0)
        loss_y()
        low_grad(2)

        @each_chunk
        def _(k):
            dpv[k] = dpv[k] + dot_nn(g_low[2], qb[Q_DN1, k])
            store_dp(k).start()

        lax.fori_loop(CHUNKS - 2, CHUNKS, rest_of_up1, 0)
        tile_copy(T_L0 + 1).start()
        loss_end()
        for i in (T_X, T_L0, T_L0 + 2):
            tile_copy(i).wait_send()
        low_grad(1)
        store_grad(1).start()

    @each_chunk
    def _(k):
        store_dp(k).wait()
        pltpu.make_async_copy(cin.at[k], block_hbm.at[k], last_sem.at[k]).wait()
        q_up(1, Q_OWN, Q_DN0, k).wait_send()

        @pl.when(outer)
        def _():
            q_up(2, Q_DN0, Q_DN1, k).wait_send()

        @pl.when(inner)
        def _():
            c_dn(k).wait_send()

    store_grad(0).wait()
    tile_copy(T_L0 + 1).wait_send()


def finish_kernel(dq, dp, blocks, grad, dq_out, dp_out, qv, pv, bv, gv, load, store):
    width = blocks.shape[2]
    rows = dq.shape[0] // CHUNKS

    def columns(k):
        return slice(k * width, (k + 1) * width)

    def piece(k):
        return slice(k * rows, (k + 1) * rows)

    copy = pltpu.make_async_copy
    loads = []
    stores = []
    first = copy(grad, gv, load.at[3, 0])
    first.start()
    for k in range(CHUNKS):
        loads.append((
            copy(dp.at[:, columns(k)], pv.at[:, columns(k)], load.at[0, k]),
            copy(blocks.at[k], bv.at[k], load.at[1, k]),
            copy(dq.at[piece(k)], qv.at[piece(k)], load.at[2, k]),
        ))
        for one in loads[-1]:
            one.start()
        stores.append((
            copy(pv.at[:, columns(k)], dp_out.at[:, columns(k)], store.at[0, k]),
            copy(qv.at[piece(k)], dq_out.at[piece(k)], store.at[1, k]),
        ))
    first.wait()
    for k in range(CHUNKS):
        for one in loads[k]:
            one.wait()
        stores[k][1].start()
        pv[:, columns(k)] = pv[:, columns(k)] + dot_nn(gv[...], bv[k])
        stores[k][0].start()
    for k in range(CHUNKS):
        for one in stores[k]:
            one.wait()


def finish(dq, dp, blocks, grad):
    anywhere = pl.BlockSpec(memory_space=pl.ANY)
    return pl.pallas_call(
        finish_kernel,
        out_shape=(jax.ShapeDtypeStruct(dq.shape, F32), jax.ShapeDtypeStruct(dp.shape, F32)),
        in_specs=[anywhere] * 4,
        out_specs=(anywhere, anywhere),
        scratch_shapes=[
            pltpu.VMEM(dq.shape, F32),
            pltpu.VMEM(dp.shape, F32),
            pltpu.VMEM(blocks.shape, BF16),
            pltpu.VMEM(grad.shape, BF16),
            pltpu.SemaphoreType.DMA((4, CHUNKS)),
            pltpu.SemaphoreType.DMA((2, CHUNKS)),
        ],
        compiler_params=pltpu.CompilerParams(vmem_limit_bytes=60 << 20),
        name="finish",
    )(dq, dp, blocks, grad)


def local(nx, ny, queries, passages, positive, pair_on):
    rows, depth = queries.shape
    width = depth // CHUNKS
    full = depth * lax.axis_size("sub")
    count = 2.0 * rows * lax.axis_size("dp")
    dma = pltpu.SemaphoreType.DMA
    block = (CHUNKS, rows, width)
    tile = (rows, rows)
    anywhere = pl.BlockSpec(memory_space=pl.ANY)
    loss, dq, dp, last_block, last_grad = pl.pallas_call(
        functools.partial(kernel, nx, ny, 1.0 / math.sqrt(full), count),
        out_shape=(
            jax.ShapeDtypeStruct((1,), F32),
            jax.ShapeDtypeStruct((rows, depth), F32),
            jax.ShapeDtypeStruct((rows, depth), F32),
            jax.ShapeDtypeStruct(block, BF16),
            jax.ShapeDtypeStruct(tile, BF16),
        ),
        in_specs=[
            anywhere,
            anywhere,
            pl.BlockSpec(memory_space=pltpu.VMEM),
            pl.BlockSpec(memory_space=pltpu.SMEM),
        ],
        out_specs=(pl.BlockSpec(memory_space=pltpu.SMEM),) + (anywhere,) * 4,
        scratch_shapes=[
            pltpu.VMEM((6,) + block, BF16),
            pltpu.VMEM((6,) + block, BF16),
            pltpu.VMEM(block, BF16),
            pltpu.VMEM(block, BF16),
            pltpu.VMEM(block, BF16),
            pltpu.VMEM((8,) + tile, F32),
            pltpu.VMEM((8,) + tile, F32),
            pltpu.VMEM(block, F32),
            pltpu.VMEM(block, F32),
            pltpu.VMEM(tile, BF16),
            pltpu.VMEM(tile, BF16),
            pltpu.VMEM((LEVELS,) + tile, BF16),
            pltpu.VMEM(tile, BF16),
            pltpu.VMEM((LEVELS,) + tile, BF16),
            pltpu.VMEM(tile, BF16),
            pltpu.VMEM((8, rows), F32),
            pltpu.VMEM((LEVELS, 8, rows), F32),
            pltpu.VMEM((LEVELS, 8, rows), F32),
            pltpu.VMEM((8, rows), F32),
            pltpu.VMEM((LEVELS + 1, 8, rows), F32),
            pltpu.VMEM((NZ, 8, 128), F32),
            pltpu.VMEM((nx, 8, 128), F32),
            pltpu.VMEM((ny, 8, 128), F32),
            dma((2, CHUNKS)),
            dma((2, CHUNKS)),
            dma((CHUNKS + 1,)),
            dma((2, CHUNKS)),
            dma((3, CHUNKS)),
            dma((5, CHUNKS)),
            dma((3, CHUNKS)),
            dma((2, CHUNKS)),
            dma((5, CHUNKS)),
            dma((2, CHUNKS)),
            dma((CHUNKS,)),
            dma((8,)),
            dma((8,)),
            dma((LEVELS,)),
            dma((LEVELS,)),
            dma((LEVELS + 1,)),
            dma((LEVELS + 1,)),
            dma((NZ,)),
            dma((NZ,)),
            dma((nx,)),
            dma((nx,)),
            dma((ny,)),
            dma((ny,)),
        ],
        compiler_params=pltpu.CompilerParams(
            collective_id=1, has_side_effects=True, vmem_limit_bytes=58 << 20
        ),
        name="infonce",
    )(queries, passages, positive, jnp.transpose(pair_on))
    dq, dp = finish(dq, dp, last_block, last_grad)
    return loss, dq, dp


def solution(mesh):
    per_z = mesh.shape["dp"] // NZ
    nx = math.isqrt(per_z)
    ny = per_z // nx
    return jax.shard_map(
        functools.partial(local, nx, ny),
        mesh=mesh,
        in_specs=(P("dp", "sub"), P("dp", "sub"), P("dp", None), P()),
        out_specs=(P(), P("dp", "sub"), P("dp", "sub")),
        check_vma=False,
    )
```

```python
import functools
import math

import jax
import jax.numpy as jnp
from jax import lax
from jax.experimental import pallas as pl
from jax.experimental.pallas import tpu as pltpu
from jax.sharding import PartitionSpec as P

MESH = pl.DeviceIdType.MESH
NZ = 8
LEVELS = 3
CHUNKS = 8
LAG = 2
SLOW = 3
EARLY = 2
FIRST = 3
NEAR = 4
F32 = jnp.float32
BF16 = jnp.bfloat16

P_UP0, P_UP1, P_UP2, P_DN0, P_DN1, P_OWN = range(6)
Q_UP0, Q_UP1, Q_DN0, Q_DN1, Q_DN2, Q_OWN = range(6)
T_OWN, T_U0, T_L0, T_X = 0, 1, 4, 7


def dot_nt(a, b):
    return lax.dot_general(a, b, (((1,), (1,)), ((), ())), preferred_element_type=F32)


def dot_nn(a, b):
    return jnp.dot(a, b, preferred_element_type=F32)


def to_lanes(column):
    rows = column.shape[0]
    return jnp.transpose(jnp.broadcast_to(column, (rows, 128)))[0:1, :]


def to_column(lanes):
    rows = lanes.shape[1]
    return jnp.transpose(jnp.broadcast_to(lanes, (128, rows)))[:, 0:1]


def lse_rows(tile):
    top = jnp.max(tile, axis=1, keepdims=True)
    return top + jnp.log(jnp.sum(jnp.exp(tile - top), axis=1, keepdims=True))


def lse_cols(tile):
    top = jnp.max(tile, axis=0, keepdims=True)
    return top + jnp.log(jnp.sum(jnp.exp(tile - top), axis=0, keepdims=True))


def kernel(
    nx, ny, scale, count,
    q_hbm, p_hbm, pos_ref, pair_ref,
    loss_ref, dq_hbm, dp_hbm, block_hbm, grad_hbm,
    pb, qb, cin, cs, cm, part, got, dqv, dpv,
    g_own, g_own_t, g_up, g_up0_t, g_low, g_x, lse,
    ms1, mr1, ms2, mr2, lz, lx, ly,
    own_sem, out_sem, last_sem,
    p_send_up, p_send_dn, p_recv,
    q_send_up, q_send_dn, q_recv,
    c_send, c_recv,
    t_send, t_recv,
    m1_send, m1_recv, m2_send, m2_recv,
    z_send, z_recv, x_send, x_recv, y_send, y_recv,
):
    rows = pb.shape[2]
    width = pb.shape[3]
    per_z = nx * ny
    dp = lax.axis_index("dp")
    sub = lax.axis_index("sub")
    z = dp // per_z
    xy = dp % per_z
    x = xy // ny
    y = xy % ny
    role = z % 4
    second = role // 2
    sign = 1 - 2 * second
    outer = (role % 3) == 0
    inner = jnp.logical_not(outer)

    def at_z(other):
        return (((other + 2 * NZ) % NZ) * per_z + xy, sub)

    up = at_z(z + sign)
    down = at_z(z - sign)
    twin = (dp, 1 - sub)

    def partner_z(level):
        step = 1 << level
        return z + step - 2 * step * ((z // step) % 2)

    partners = [at_z(partner_z(level)) for level in range(LEVELS)]
    far2 = at_z(z - 2 * sign)

    def remote(src, dst, send, recv, device):
        return pltpu.make_async_remote_copy(
            src_ref=src, dst_ref=dst, send_sem=send, recv_sem=recv,
            device_id=device, device_id_type=MESH,
        )

    def p_up(i, src, dst, k):
        return remote(pb.at[src, k], pb.at[dst, k], p_send_up.at[i, k], p_recv.at[dst, k], up)

    def p_dn(i, src, dst, k):
        return remote(pb.at[src, k], pb.at[dst, k], p_send_dn.at[i, k], p_recv.at[dst, k], down)

    def q_up(i, src, dst, k):
        return remote(qb.at[src, k], qb.at[dst, k], q_send_up.at[i, k], q_recv.at[dst, k], up)

    def q_dn(i, src, dst, k):
        return remote(qb.at[src, k], qb.at[dst, k], q_send_dn.at[i, k], q_recv.at[dst, k], down)

    def c_up(k):
        return remote(cs.at[k], cin.at[k], c_send.at[0, k], c_recv.at[k], up)

    def c_dn(k):
        return remote(cm.at[k], cin.at[k], c_send.at[1, k], c_recv.at[k], down)

    def p_wait(slot, k):
        remote(pb.at[slot, k], pb.at[slot, k], p_send_up.at[0, k], p_recv.at[slot, k], up).wait_recv()

    def q_wait(slot, k):
        remote(qb.at[slot, k], qb.at[slot, k], q_send_up.at[0, k], q_recv.at[slot, k], up).wait_recv()

    def tile_copy(i):
        return remote(part.at[i], got.at[i], t_send.at[i], t_recv.at[i], twin)

    def finish_tile(i):
        tile_copy(i).wait_recv()
        got[i] = (got[i] + part[i]) * scale

    def m1_copy(level):
        return remote(ms1.at[level], mr1.at[level], m1_send.at[level], m1_recv.at[level], partners[level])

    def m2_copy(i):
        device = partners[i] if i < LEVELS else far2
        return remote(ms2, mr2.at[i], m2_send.at[i], m2_recv.at[i], device)

    def z_copy(d):
        return remote(lz.at[z], lz.at[z], z_send.at[d], z_recv.at[z], at_z(z + d))

    def z_wait(d):
        other = (z + d) % NZ
        remote(lz.at[other], lz.at[other], z_send.at[d], z_recv.at[other], at_z(z + d)).wait_recv()

    def x_device(d):
        return (z * per_z + ((x + d) % nx) * ny + y, sub)

    def x_copy(d):
        return remote(lx.at[x], lx.at[x], x_send.at[d], x_recv.at[x], x_device(d))

    def x_wait(d):
        other = (x + d) % nx
        remote(lx.at[other], lx.at[other], x_send.at[d], x_recv.at[other], x_device(d)).wait_recv()

    def y_device(d):
        return (z * per_z + x * ny + (y + d) % ny, sub)

    def y_copy(d):
        return remote(ly.at[y], ly.at[y], y_send.at[d], y_recv.at[y], y_device(d))

    def y_wait(d):
        other = (y + d) % ny
        remote(ly.at[other], ly.at[other], y_send.at[d], y_recv.at[other], y_device(d)).wait_recv()

    def load_p(k):
        return pltpu.make_async_copy(
            p_hbm.at[:, pl.ds(pl.multiple_of(k * width, width), width)], pb.at[P_OWN, k], own_sem.at[0, k]
        )

    def load_q(k):
        return pltpu.make_async_copy(
            q_hbm.at[:, pl.ds(pl.multiple_of(k * width, width), width)], qb.at[Q_OWN, k], own_sem.at[1, k]
        )

    def store_dq(k):
        return pltpu.make_async_copy(
            dqv.at[k], dq_hbm.at[:, pl.ds(pl.multiple_of(k * width, width), width)], out_sem.at[0, k]
        )

    def store_dp(k):
        return pltpu.make_async_copy(
            dpv.at[k], dp_hbm.at[:, pl.ds(pl.multiple_of(k * width, width), width)], out_sem.at[1, k]
        )

    def store_block(k):
        @pl.when(outer)
        def _():
            pltpu.make_async_copy(cin.at[k], block_hbm.at[k], last_sem.at[k]).start()

        @pl.when(inner)
        def _():
            pltpu.make_async_copy(qb.at[Q_UP1, k], block_hbm.at[k], last_sem.at[k]).start()

    def store_grad(i):
        return pltpu.make_async_copy(g_low.at[i], grad_hbm, last_sem.at[CHUNKS])

    def each_chunk(body):
        def step(k, carry):
            body(k)
            return carry

        lax.fori_loop(0, CHUNKS, step, 0)

    def each_step(body):
        def step(k, carry):
            body(k)
            return carry

        lax.fori_loop(0, CHUNKS + LAG, step, 0)

    def add_tile(i, k, left, right):
        @pl.when(k == 0)
        def _():
            part[i] = dot_nt(left, right)

        @pl.when(k > 0)
        def _():
            part[i] = part[i] + dot_nt(left, right)

    barrier = pltpu.get_barrier_semaphore()
    greeted = [twin]
    greeted += [at_z(z + d) for d in range(1, NZ)]
    greeted += [x_device(d) for d in range(1, nx)]
    greeted += [y_device(d) for d in range(1, ny)]
    for device in greeted:
        pl.semaphore_signal(barrier, inc=1, device_id=device, device_id_type=MESH)

    @each_chunk
    def _(k):
        load_p(k).start()

    @each_chunk
    def _(k):
        load_q(k).start()

    pl.semaphore_wait(barrier, len(greeted))

    @each_chunk
    def _(k):
        load_p(k).wait()

        @pl.when(outer)
        def _():
            p_up(0, P_OWN, P_DN0, k).start()

        @pl.when(inner)
        def _():
            p_up(0, P_OWN, P_UP0, k).start()

            @pl.when(k < EARLY)
            def _():
                p_dn(0, P_OWN, P_UP0, k).start()

    @each_chunk
    def _(k):
        load_q(k).wait()

    near = jnp.where(outer, P_UP0, P_DN0)
    active = [pair_ref[level, dp] > 0 for level in range(LEVELS)]
    x_active = pair_ref[2, partner_z(1) * per_z + xy] > 0

    def add_up(level, slot, k):
        add_tile(T_U0 + level, k, qb[Q_OWN, k], pb[slot, k])

    def add_low(level, slot, k):
        add_tile(T_L0 + level, k, pb[P_OWN, k], qb[slot, k])

    def add_own(k):
        add_tile(T_OWN, k, pb[P_OWN, k], qb[Q_OWN, k])

    def up_stats(level):
        finish_tile(T_U0 + level)
        tile = got[T_U0 + level]
        ms1[level] = jnp.broadcast_to(lse_cols(tile), (8, rows))
        m1_copy(level).start()
        lse[2 + level:3 + level, :] = to_lanes(lse_rows(tile))

    def own_stats():
        finish_tile(T_OWN)
        lse[0:1, :] = lse_cols(got[T_OWN])
        lse[1:2, :] = to_lanes(lse_rows(got[T_OWN]))

    def gather(parts):
        parts = [parts[0]] + [jnp.where(a, v, -jnp.inf) for a, v in zip(active, parts[1:])]
        top = functools.reduce(jnp.maximum, parts)
        return top + jnp.log(functools.reduce(jnp.add, [jnp.exp(v - top) for v in parts]))

    def all_stats():
        for level in range(LEVELS):
            m1_copy(level).wait_recv()
        row_lse = gather([lse[0:1, :]] + [lse[2 + level:3 + level, :] for level in range(LEVELS)])
        col_lse = gather([lse[1:2, :]] + [mr1[level][0:1, :] for level in range(LEVELS)])
        lse[5:6, :] = row_lse
        lse[6:7, :] = col_lse
        ms2[0:4, :] = jnp.broadcast_to(row_lse, (4, rows))
        ms2[4:8, :] = jnp.broadcast_to(col_lse, (4, rows))
        for level in range(LEVELS):
            m2_copy(level).start()

    def hits():
        return (pos_ref[...] == lax.broadcasted_iota(jnp.int32, (rows, rows), 0)).astype(F32)

    def loss_start():
        share = jnp.sum(lse[5:7, :]) - 2.0 * jnp.sum(got[T_OWN] * hits())
        lz[z] = jnp.full((8, 128), share, F32)
        for d in range(1, NZ):
            z_copy(d).start()

    def loss_x():
        for d in range(1, NZ):
            z_wait(d)
        lx[x] = functools.reduce(jnp.add, [lz[i] for i in range(NZ)])
        for d in range(1, nx):
            x_copy(d).start()

    def loss_y():
        for d in range(1, nx):
            x_wait(d)
        ly[y] = functools.reduce(jnp.add, [lx[i] for i in range(nx)])
        for d in range(1, ny):
            y_copy(d).start()

    def own_grads():
        tile = got[T_OWN]
        grad = jnp.exp(tile - lse[5:6, :]) + jnp.exp(tile - to_column(lse[6:7, :])) - 2.0 * hits()
        g_own_t[...] = grad.astype(BF16)
        g_own[...] = jnp.transpose(grad).astype(BF16)

    def up_grad(level, also_t=False):
        tile = got[T_U0 + level]
        grad = jnp.exp(tile - to_column(lse[5:6, :])) + jnp.exp(tile - mr2[level][4:5, :])
        grad = jnp.where(active[level], grad, 0.0)
        g_up[level] = grad.astype(BF16)
        if also_t:
            g_up0_t[...] = jnp.transpose(grad).astype(BF16)

    def low_grad(level):
        finish_tile(T_L0 + level)
        tile = got[T_L0 + level]
        grad = jnp.exp(tile - mr2[level][0:1, :]) + jnp.exp(tile - to_column(lse[6:7, :]))
        g_low[level] = jnp.where(active[level], grad, 0.0).astype(BF16)

    def c_wait(k):
        remote(cs.at[k], cin.at[k], c_send.at[0, k], c_recv.at[k], up).wait_recv()

    def settle():
        @each_chunk
        def _(k):
            store_dq(k).wait()
            p_up(0, P_OWN, P_DN0, k).wait_send()
            p_up(1, P_DN0, P_DN1, k).wait_send()
            p_dn(0, P_UP1, P_DN0, k).wait_send()
            p_dn(1, P_UP2, P_DN1, k).wait_send()
            q_up(0, Q_DN2, Q_DN2, k).wait_send()
            q_dn(0, Q_OWN, Q_DN2, k).wait_send()

        tile_copy(T_OWN).wait_send()
        for level in range(LEVELS):
            tile_copy(T_U0 + level).wait_send()
            m1_copy(level).wait_send()
            m2_copy(level).wait_send()
        for d in range(1, NZ):
            z_copy(d).wait_send()

    def loss_end():
        for d in range(1, ny):
            y_wait(d)
        total_loss = functools.reduce(jnp.add, [ly[i] for i in range(ny)])
        loss_ref[0] = jnp.max(total_loss) / count
        for d in range(1, nx):
            x_copy(d).wait_send()
        for d in range(1, ny):
            y_copy(d).wait_send()

    def query_grad(k):
        total = dot_nn(g_own[...], pb[P_OWN, k])
        total = total + dot_nn(g_up[0], pb[near, k])
        total = total + dot_nn(g_up[1], pb[P_UP1, k])
        dqv[k] = total + dot_nn(g_up[2], pb[P_DN1, k])
        store_dq(k).start()

    def q_far(k):
        q_wait(Q_DN2, k)
        q_up(0, Q_DN2, Q_DN2, k).start()

    def at(k, step, body):
        pl.when(k == step)(body)

    @pl.when(outer)
    def _():
        for k in range(FIRST):
            q_dn(0, Q_OWN, Q_DN2, k).start()

        @each_step
        def _(k):
            @pl.when(k < CHUNKS)
            def _():
                p_wait(P_UP1, k)
                p_dn(0, P_UP1, P_DN0, k).start()
                add_up(1, P_UP1, k)

            @pl.when(k >= LAG)
            def _():
                p_wait(P_DN0, k - LAG)
                p_up(1, P_DN0, P_DN1, k - LAG).start()

        tile_copy(T_U0 + 1).start()
        for k in range(NEAR):
            q_up(1, Q_OWN, Q_DN0, k).start()
        for k in range(EARLY):
            q_far(k)

        @each_step
        def _(k):
            @pl.when(k < CHUNKS)
            def _():
                p_wait(P_UP2, k)
                p_dn(1, P_UP2, P_DN1, k).start()
                add_own(k)

            @pl.when(k >= LAG)
            def _():
                p_wait(P_DN1, k - LAG)
                add_up(2, P_DN1, k - LAG)

            at(k, 2, lambda: up_stats(1))

            @pl.when(k == CHUNKS - 1)
            def _():
                for j in range(FIRST, CHUNKS):
                    q_dn(0, Q_OWN, Q_DN2, j).start()

        tile_copy(T_OWN).start()
        tile_copy(T_U0 + 2).start()
        own_stats()
        up_stats(2)

        @each_chunk
        def _(k):
            p_wait(P_UP0, k)
            add_up(0, P_UP0, k)

            @pl.when(k >= EARLY + LAG)
            def _():
                q_far(k - LAG)

        tile_copy(T_U0).start()
        up_stats(0)
        q_far(CHUNKS - LAG)
        all_stats()
        m2_copy(LEVELS).start()
        for k in range(CHUNKS - LAG + 1, CHUNKS):
            q_far(k)
        for k in range(NEAR, CHUNKS):
            q_up(1, Q_OWN, Q_DN0, k).start()

        @each_step
        def _(k):
            @pl.when(k < CHUNKS)
            def _():
                q_wait(Q_UP1, k)
                q_dn(1, Q_UP1, Q_DN0, k).start()
                add_low(1, Q_UP1, k)

            @pl.when(k >= LAG)
            def _():
                q_wait(Q_DN0, k - LAG)
                q_up(2, Q_DN0, Q_DN1, k - LAG).start()

            at(k, 2, loss_start)
            at(k, 3, own_grads)

        tile_copy(T_L0 + 1).start()
        for level in range(LEVELS):
            m2_copy(level).wait_recv()
            up_grad(level)
        low_grad(1)
        loss_x()

        @each_chunk
        def _(k):
            query_grad(k)
            dpv[k] = dot_nn(g_own_t[...], qb[Q_OWN, k]) + dot_nn(g_low[1], qb[Q_UP1, k])
            store_dp(k).start()

        i = lax.broadcasted_iota(jnp.int32, (rows, rows), 0)
        j = lax.broadcasted_iota(jnp.int32, (rows, rows), 1)
        g_low[0] = (i == j).astype(F32).astype(BF16)
        store_grad(0).start()
        loss_y()
        settle()
        loss_end()
        m2_copy(LEVELS).wait_send()

        @each_chunk
        def _(k):
            q_dn(1, Q_UP1, Q_DN0, k).wait_send()

        @each_chunk
        def _(k):
            c_wait(k)
            store_block(k)

    @pl.when(inner)
    def _():
        @each_chunk
        def _(k):
            p_wait(P_UP0, k)
            p_dn(1, P_UP0, P_UP1, k).start()
            p_wait(P_DN0, k)
            p_up(1, P_DN0, P_UP1, k).start()
            add_up(0, P_DN0, k)

        tile_copy(T_U0).start()

        @each_chunk
        def _(k):
            q_up(0, Q_OWN, Q_UP0, k).start()

        @each_chunk
        def _(k):
            p_wait(P_UP1, k)
            p_dn(2, P_UP1, P_UP2, k).start()
            add_up(1, P_UP1, k)

        for k in range(EARLY, CHUNKS):
            p_dn(0, P_OWN, P_UP0, k).start()
        tile_copy(T_U0 + 1).start()

        @each_chunk
        def _(k):
            add_own(k)
            p_wait(P_DN1, k)
            add_up(2, P_DN1, k)

        tile_copy(T_OWN).start()
        tile_copy(T_U0 + 2).start()
        up_stats(0)
        up_stats(1)
        up_stats(2)
        own_stats()

        @each_chunk
        def _(k):
            q_wait(Q_UP0, k)
            q_dn(0, Q_UP0, Q_UP1, k).start()

            @pl.when(k < NEAR)
            def _():
                q_wait(Q_DN0, k)
                q_up(1, Q_DN0, Q_UP1, k).start()
                add_low(0, Q_DN0, k)

        def add_x(k):
            q_wait(Q_DN2, k)
            add_tile(T_X, k, pb[P_UP1, k], qb[Q_DN2, k])

        @each_chunk
        def _(k):
            add_x(k)
            at(k, CHUNKS - 2, all_stats)
            at(k, CHUNKS - 2, loss_start)

        tile_copy(T_X).start()
        finish_tile(T_X)
        m2_copy(1).wait_recv()
        m2_copy(LEVELS).wait_recv()
        tile = got[T_X]
        grad = jnp.exp(tile - mr2[LEVELS][0:1, :]) + jnp.exp(tile - to_column(mr2[1][4:5, :]))
        g_x[...] = jnp.where(x_active, grad, 0.0).astype(BF16)

        @each_chunk
        def _(k):
            cs[k] = dot_nn(g_x[...], qb[Q_DN2, k]).astype(BF16)
            c_up(k).start()

        m2_copy(0).wait_recv()
        up_grad(0, True)
        up_grad(1)
        m2_copy(2).wait_recv()
        up_grad(2)
        own_grads()

        @each_step
        def _(k):
            @pl.when(k < CHUNKS)
            def _():
                c_wait(k)
                cm[k] = (cin[k].astype(F32) + dot_nn(g_up0_t[...], qb[Q_OWN, k])).astype(BF16)
                c_dn(k).start()

            @pl.when(jnp.logical_and(k >= 1, k < 1 + CHUNKS - NEAR))
            def _():
                late = NEAR + k - 1
                q_wait(Q_DN0, late)
                q_up(1, Q_DN0, Q_UP1, late).start()
                add_low(0, Q_DN0, late)

            @pl.when(k < CHUNKS)
            def _():
                query_grad(k)
                dpv[k] = dot_nn(g_own_t[...], qb[Q_OWN, k])

            @pl.when(jnp.logical_and(k >= 2, k < 2 + NEAR))
            def _():
                q_wait(Q_UP1, k - 2)
                store_block(k - 2)
                add_low(1, Q_UP1, k - 2)

            at(k, CHUNKS - NEAR + 1, lambda: tile_copy(T_L0).start())
            at(k, CHUNKS - NEAR + 2, lambda: low_grad(0))

            @pl.when(k >= SLOW)
            def _():
                q_wait(Q_DN1, k - SLOW)
                add_low(2, Q_DN1, k - SLOW)

        @each_chunk
        def _(k):
            dpv[k] = dpv[k] + dot_nn(g_low[0], qb[Q_DN0, k])

        loss_x()

        def rest_of_dn1(k, carry):
            q_wait(Q_DN1, k)
            add_low(2, Q_DN1, k)
            return carry

        lax.fori_loop(CHUNKS + LAG - SLOW, CHUNKS, rest_of_dn1, 0)
        tile_copy(T_L0 + 2).start()
        settle()

        @each_chunk
        def _(k):
            p_dn(2, P_UP1, P_UP2, k).wait_send()
            c_up(k).wait_send()

        def rest_of_up1(k, carry):
            q_wait(Q_UP1, k)
            store_block(k)
            add_low(1, Q_UP1, k)
            return carry

        lax.fori_loop(NEAR, CHUNKS - 2, rest_of_up1, 0)
        loss_y()
        low_grad(2)

        @each_chunk
        def _(k):
            dpv[k] = dpv[k] + dot_nn(g_low[2], qb[Q_DN1, k])
            store_dp(k).start()

        lax.fori_loop(CHUNKS - 2, CHUNKS, rest_of_up1, 0)
        tile_copy(T_L0 + 1).start()
        loss_end()
        for i in (T_X, T_L0, T_L0 + 2):
            tile_copy(i).wait_send()
        low_grad(1)
        store_grad(1).start()

    @each_chunk
    def _(k):
        store_dp(k).wait()
        pltpu.make_async_copy(cin.at[k], block_hbm.at[k], last_sem.at[k]).wait()
        q_up(1, Q_OWN, Q_DN0, k).wait_send()

        @pl.when(outer)
        def _():
            q_up(2, Q_DN0, Q_DN1, k).wait_send()

        @pl.when(inner)
        def _():
            c_dn(k).wait_send()

    store_grad(0).wait()
    tile_copy(T_L0 + 1).wait_send()


def finish_kernel(dq, dp, blocks, grad, dq_out, dp_out, qv, pv, bv, gv, load, store):
    width = blocks.shape[2]
    rows = dq.shape[0] // CHUNKS

    def columns(k):
        return slice(k * width, (k + 1) * width)

    def piece(k):
        return slice(k * rows, (k + 1) * rows)

    copy = pltpu.make_async_copy
    loads = []
    stores = []
    first = copy(grad, gv, load.at[3, 0])
    first.start()
    for k in range(CHUNKS):
        loads.append((
            copy(dp.at[:, columns(k)], pv.at[:, columns(k)], load.at[0, k]),
            copy(blocks.at[k], bv.at[k], load.at[1, k]),
            copy(dq.at[piece(k)], qv.at[piece(k)], load.at[2, k]),
        ))
        for one in loads[-1]:
            one.start()
        stores.append((
            copy(pv.at[:, columns(k)], dp_out.at[:, columns(k)], store.at[0, k]),
            copy(qv.at[piece(k)], dq_out.at[piece(k)], store.at[1, k]),
        ))
    first.wait()
    for k in range(CHUNKS):
        for one in loads[k]:
            one.wait()
        stores[k][1].start()
        pv[:, columns(k)] = pv[:, columns(k)] + dot_nn(gv[...], bv[k])
        stores[k][0].start()
    for k in range(CHUNKS):
        for one in stores[k]:
            one.wait()


def finish(dq, dp, blocks, grad):
    anywhere = pl.BlockSpec(memory_space=pl.ANY)
    return pl.pallas_call(
        finish_kernel,
        out_shape=(jax.ShapeDtypeStruct(dq.shape, F32), jax.ShapeDtypeStruct(dp.shape, F32)),
        in_specs=[anywhere] * 4,
        out_specs=(anywhere, anywhere),
        scratch_shapes=[
            pltpu.VMEM(dq.shape, F32),
            pltpu.VMEM(dp.shape, F32),
            pltpu.VMEM(blocks.shape, BF16),
            pltpu.VMEM(grad.shape, BF16),
            pltpu.SemaphoreType.DMA((4, CHUNKS)),
            pltpu.SemaphoreType.DMA((2, CHUNKS)),
        ],
        compiler_params=pltpu.CompilerParams(vmem_limit_bytes=60 << 20),
        name="finish",
    )(dq, dp, blocks, grad)


def local(nx, ny, queries, passages, positive, pair_on):
    rows, depth = queries.shape
    width = depth // CHUNKS
    full = depth * lax.axis_size("sub")
    count = 2.0 * rows * lax.axis_size("dp")
    dma = pltpu.SemaphoreType.DMA
    block = (CHUNKS, rows, width)
    tile = (rows, rows)
    anywhere = pl.BlockSpec(memory_space=pl.ANY)
    loss, dq, dp, last_block, last_grad = pl.pallas_call(
        functools.partial(kernel, nx, ny, 1.0 / math.sqrt(full), count),
        out_shape=(
            jax.ShapeDtypeStruct((1,), F32),
            jax.ShapeDtypeStruct((rows, depth), F32),
            jax.ShapeDtypeStruct((rows, depth), F32),
            jax.ShapeDtypeStruct(block, BF16),
            jax.ShapeDtypeStruct(tile, BF16),
        ),
        in_specs=[
            anywhere,
            anywhere,
            pl.BlockSpec(memory_space=pltpu.VMEM),
            pl.BlockSpec(memory_space=pltpu.SMEM),
        ],
        out_specs=(pl.BlockSpec(memory_space=pltpu.SMEM),) + (anywhere,) * 4,
        scratch_shapes=[
            pltpu.VMEM((6,) + block, BF16),
            pltpu.VMEM((6,) + block, BF16),
            pltpu.VMEM(block, BF16),
            pltpu.VMEM(block, BF16),
            pltpu.VMEM(block, BF16),
            pltpu.VMEM((8,) + tile, F32),
            pltpu.VMEM((8,) + tile, F32),
            pltpu.VMEM(block, F32),
            pltpu.VMEM(block, F32),
            pltpu.VMEM(tile, BF16),
            pltpu.VMEM(tile, BF16),
            pltpu.VMEM((LEVELS,) + tile, BF16),
            pltpu.VMEM(tile, BF16),
            pltpu.VMEM((LEVELS,) + tile, BF16),
            pltpu.VMEM(tile, BF16),
            pltpu.VMEM((8, rows), F32),
            pltpu.VMEM((LEVELS, 8, rows), F32),
            pltpu.VMEM((LEVELS, 8, rows), F32),
            pltpu.VMEM((8, rows), F32),
            pltpu.VMEM((LEVELS + 1, 8, rows), F32),
            pltpu.VMEM((NZ, 8, 128), F32),
            pltpu.VMEM((nx, 8, 128), F32),
            pltpu.VMEM((ny, 8, 128), F32),
            dma((2, CHUNKS)),
            dma((2, CHUNKS)),
            dma((CHUNKS + 1,)),
            dma((2, CHUNKS)),
            dma((3, CHUNKS)),
            dma((5, CHUNKS)),
            dma((3, CHUNKS)),
            dma((2, CHUNKS)),
            dma((5, CHUNKS)),
            dma((2, CHUNKS)),
            dma((CHUNKS,)),
            dma((8,)),
            dma((8,)),
            dma((LEVELS,)),
            dma((LEVELS,)),
            dma((LEVELS + 1,)),
            dma((LEVELS + 1,)),
            dma((NZ,)),
            dma((NZ,)),
            dma((nx,)),
            dma((nx,)),
            dma((ny,)),
            dma((ny,)),
        ],
        compiler_params=pltpu.CompilerParams(
            collective_id=1, has_side_effects=True, vmem_limit_bytes=58 << 20
        ),
        name="infonce",
    )(queries, passages, positive, jnp.transpose(pair_on))
    dq, dp = finish(dq, dp, last_block, last_grad)
    return loss, dq, dp


def solution(mesh):
    per_z = mesh.shape["dp"] // NZ
    nx = math.isqrt(per_z)
    ny = per_z // nx
    return jax.shard_map(
        functools.partial(local, nx, ny),
        mesh=mesh,
        in_specs=(P("dp", "sub"), P("dp", "sub"), P("dp", None), P()),
        out_specs=(P(), P("dp", "sub"), P("dp", "sub")),
        check_vma=False,
    )
```
